32 devices in a mesh: groups: 2 (over y), ctx: 8 (over z, x), head: 2 (over core).
Axes of the slice: x: 2, y: 2, z: 4, core: 2. Of those that a mesh axis runs over, the one named last changes fastest.
Arguments:
- queries: bfloat16 [4096, 512], P(('groups', 'ctx'), 'head'), parts along dimension 0, may hold values from -5 to 5
- key_input: bfloat16 [4096, 128], P(('groups', 'ctx')), parts along dimension 0, may hold values from -5 to 5
- value_input: bfloat16 [4096, 128], P(('groups', 'ctx')), parts along dimension 0, may hold values from -2.5 to 2.5
- grad_out: bfloat16 [4096, 512], P(('groups', 'ctx'), 'head'), parts along dimension 0, may hold values from -1.5 to 1.5
- doc_lengths: int32 [32], P('groups'), parts along dimension 0, may hold values from 1 to 512, 2048 in all
- stretch_plan: int32 [32], P(('groups', 'ctx')), parts along dimension 0, may hold values from 0 to 15, as said below
Outputs:
- output: bfloat16 [4096, 512], P(('groups', 'ctx'), 'head'), parts along dimension 0
- query_grad: float32 [4096, 512], P(('groups', 'ctx'), 'head'), parts along dimension 0
- key_grad: float32 [4096, 128], P(('groups', 'ctx')), parts along dimension 0
- value_grad: float32 [4096, 128], P(('groups', 'ctx')), parts along dimension 0
The draws below stay inside these ranges and needn't reach their ends.
There are 2 independent parts, one for each index of `groups`. The reference program is written for one: setup_inputs(seed, part) draws one part's arguments, and reference() takes and returns one part's arrays. A program takes and returns all parts, laid end to end along the dimension named above; each array names one. Nothing has to cross between parts.
Inputs may be any that keep to these rules, and one draw needn't show every extreme that they name: A permutation of the stretch numbers: slot j holds stretch stretch_plan[j], and |stretch_plan[j] - j| <= 4 for every slot, with equality for some slot.
All inputs are finite; a program needn't handle non-finite values.
Results may differ from the reference program's by a relative error of at most 0.025.
Values may be sent and summed in bfloat16 or wider, within the bound.
A program may use at most 64 MiB of HBM per device.

```python
import math
import jax
import jax.numpy as jnp
import numpy as np
from jax import lax

DH = 128
QHEADS = 4
TOK_DEV = 256
HOPS = 2
TOKENS = 2048
STRETCH = 128
STRETCHES = 16
DOC_MAX = 512
DOCS = 16
N_CTX = 8


def draw_queries(key, part):
    drawn = jax.random.normal(jax.random.fold_in(key, 1), (TOKENS, QHEADS * DH))
    return jnp.clip(drawn, -4.5, 4.5).astype(jnp.bfloat16)


def draw_key_input(key, part):
    drawn = jax.random.normal(jax.random.fold_in(key, 2), (TOKENS, DH))
    return jnp.clip(drawn, -4.5, 4.5).astype(jnp.bfloat16)


def draw_stretch_plan(key, part):
    spread = 2 * HOPS
    numbers = jnp.arange(STRETCHES, dtype=jnp.int32)
    noise = jax.random.randint(jax.random.fold_in(key, 3), (STRETCHES,), 0, spread + 2)
    noise = jnp.where(numbers == 0, spread + 1, jnp.where(numbers <= spread + 1, 0, noise))
    far_end = STRETCHES - 1 - spread
    noise = jnp.where(numbers == far_end, spread + 1, jnp.where(numbers > far_end, 0, noise))
    ranking = (numbers + noise) * STRETCHES + numbers
    return jnp.argsort(ranking).astype(jnp.int32)


def block_levels(own_key, extent, shards, smallest, top_value):
    gain = 1.0
    for axis_at, parts in shards:
        draws = jax.random.uniform(jax.random.fold_in(jax.random.fold_in(own_key, 6), axis_at), (parts,), jnp.float32, smallest / len(shards), top_value / len(shards))
        gain = gain * jnp.repeat(jnp.exp(draws), extent[axis_at] // parts).reshape((-1,) + (1,) * (len(extent) - 1 - axis_at))
    return gain


def length_profile(number_of, total, most, lean):
    portions = [(1 << 20) // math.isqrt(rank ** lean) + 1 for rank in range(2, number_of + 1)]
    rest, given = total - most - (number_of - 1), [1] * (number_of - 1)
    while rest > 0:
        candidates = [i for i in range(number_of - 1) if given[i] < most]
        mass, left = sum([portions[i] for i in candidates]), rest
        for i in candidates:
            extra = min(most - given[i], max(1, left * portions[i] // mass), rest)
            given[i] = given[i] + extra
            rest = rest - extra
    return np.array([most] + given)


def uneven_parts(rng, count, total, bound, lean):
    if count == 2:
        one = jax.random.randint(rng, (), max(1, total - bound), min(bound, total - 1) + 1)
        return jnp.stack([one, total - one])
    tallies = jnp.asarray(length_profile(count, total, bound, lean), jnp.int32)
    couples = (count - 1) // 2
    source_of, sink = tallies[1:1 + 2 * couples:2], tallies[2:2 + 2 * couples:2]
    margin = jnp.minimum(source_of - 1, bound - sink)
    shifted = jax.random.randint(jax.random.fold_in(rng, 1), (couples,), 0, 1 << 20) % (margin + 1)
    tallies = tallies.at[1:1 + 2 * couples:2].set(source_of - shifted).at[2:2 + 2 * couples:2].set(sink + shifted)
    return tallies[jax.random.permutation(jax.random.fold_in(rng, 2), count)]


def gaussian(key, extent, scale, reach, pieces=(), kind=jnp.bfloat16):
    drawn = scale * jax.random.normal(key, extent, jnp.float32)
    if pieces:
        drawn = drawn * block_levels(key, extent, pieces, -0.22, 0.18)
    return jnp.clip(drawn, -reach, reach).astype(kind)


def setup_inputs(seed: int = 0, part: int = 0) -> dict:
    splits = jax.random.split(jax.random.key(seed), 7)
    own_keys = jax.random.split(jax.random.fold_in(splits[6], part), 7)
    queries = draw_queries(jax.random.fold_in(jax.random.fold_in(splits[6], part), 71), part)
    key_input = draw_key_input(jax.random.fold_in(jax.random.fold_in(splits[6], part), 71), part)
    value_input = gaussian(own_keys[2], (TOKENS, DH), 0.5, 2.5, ((0, 8),))
    grad_out = gaussian(own_keys[3], (TOKENS, QHEADS * DH), 0.25, 1.5, ((0, 8), (1, 2)))
    doc_lengths = uneven_parts(own_keys[4], DOCS, TOKENS, DOC_MAX, 2).astype(jnp.int32)
    stretch_plan = draw_stretch_plan(jax.random.fold_in(jax.random.fold_in(splits[6], part), 71), part)
    return dict(queries=queries, key_input=key_input, value_input=value_input, grad_out=grad_out, doc_lengths=doc_lengths, stretch_plan=stretch_plan)


neg_large = -1e+30

def doc_numbers(bounds, places):
    return lax.optimization_barrier(jnp.sum((bounds[None, :] <= places[:, None]).astype(jnp.int32), axis=1))

def rounded(values_f32):
    return lax.optimization_barrier(values_f32.astype(jnp.bfloat16)).astype(jnp.float32)

def reference(queries, key_input, value_input, grad_out, doc_lengths, stretch_plan):
    inv_root = 1.0 / math.sqrt(DH)
    bounds = jnp.cumsum(doc_lengths).astype(jnp.int32)
    places = jnp.arange(TOKENS, dtype=jnp.int32)
    docs = doc_numbers(bounds, places)
    front = DOC_MAX
    key_padded = jnp.concatenate([jnp.zeros((front, DH), jnp.float32), key_input.astype(jnp.float32)], axis=0)
    value_padded = jnp.concatenate([jnp.zeros((front, DH), jnp.float32), value_input.astype(jnp.float32)], axis=0)
    docs_padded = jnp.concatenate([jnp.full((front,), -1, jnp.int32), docs])
    query_heads = queries.reshape(TOKENS, QHEADS, DH)
    grad_heads = grad_out.reshape(TOKENS, QHEADS, DH)
    key_width = front + TOK_DEV

    def one_block(carried, block_number):
        key_total, value_total = carried
        row_start = (block_number * TOK_DEV).astype(jnp.int32)
        query_block = lax.dynamic_slice_in_dim(query_heads, row_start, TOK_DEV, 0).astype(jnp.float32)
        grad_block = lax.dynamic_slice_in_dim(grad_heads, row_start, TOK_DEV, 0).astype(jnp.float32)
        query_places = row_start + jnp.arange(TOK_DEV, dtype=jnp.int32)
        query_docs = lax.dynamic_slice_in_dim(docs, row_start, TOK_DEV, 0)
        key_block = lax.dynamic_slice_in_dim(key_padded, row_start, key_width, 0)
        value_block = lax.dynamic_slice_in_dim(value_padded, row_start, key_width, 0)
        key_docs = lax.dynamic_slice_in_dim(docs_padded, row_start, key_width, 0)
        key_places = row_start - front + jnp.arange(key_width, dtype=jnp.int32)
        allowed = (query_docs[:, None] == key_docs[None, :]) & (key_places[None, :] <= query_places[:, None])
        scores = jnp.einsum('phd,td->pht', query_block, key_block) * inv_root
        scores = jnp.where(allowed[:, None, :], scores, neg_large)
        row_top = lax.optimization_barrier(jnp.max(scores, axis=2))
        row_total = lax.optimization_barrier(jnp.sum(jnp.where(allowed[:, None, :], jnp.exp(scores - row_top[:, :, None]), 0.0), axis=2))
        log_total = row_top + jnp.log(row_total)
        weights = jnp.where(allowed[:, None, :], jnp.exp(scores - log_total[:, :, None]), 0.0)
        weights_b = rounded(weights)
        attended = jnp.einsum('pht,td->phd', weights_b, value_block).astype(jnp.bfloat16)
        row_dots = lax.optimization_barrier(jnp.sum(grad_block * attended.astype(jnp.float32), axis=2))
        grad_weights = jnp.einsum('phd,td->pht', grad_block, value_block)
        grad_scores = rounded(weights * (grad_weights - row_dots[:, :, None]))
        query_nat = jnp.einsum('pht,td->phd', grad_scores, key_block) * inv_root
        key_part = jnp.einsum('pht,phd->td', grad_scores, query_block)
        value_part = jnp.einsum('pht,phd->td', weights_b, grad_block)
        key_total = lax.dynamic_update_slice_in_dim(key_total, lax.dynamic_slice_in_dim(key_total, row_start, key_width, 0) + key_part, row_start, 0)
        value_total = lax.dynamic_update_slice_in_dim(value_total, lax.dynamic_slice_in_dim(value_total, row_start, key_width, 0) + value_part, row_start, 0)
        return ((key_total, value_total), (attended, query_nat))
    zeros_pad = jnp.zeros((TOKENS + front, DH), jnp.float32)
    totals, outputs = lax.scan(one_block, (zeros_pad, zeros_pad), jnp.arange(N_CTX, dtype=jnp.int32))
    key_total, value_total = totals
    attended_all = outputs[0].reshape(STRETCHES, STRETCH, QHEADS * DH)
    query_all = outputs[1].reshape(STRETCHES, STRETCH, QHEADS * DH)
    output = attended_all[stretch_plan].reshape(TOKENS, QHEADS * DH)
    query_grad = query_all[stretch_plan].reshape(TOKENS, QHEADS * DH)
    key_grad = key_total[front:] * inv_root
    value_grad = value_total[front:]
    return (output, query_grad, key_grad, value_grad)
```

```python
import functools
import math

import jax
import jax.numpy as jnp
from jax import lax
from jax.experimental import pallas as pl
from jax.experimental.pallas import tpu as pltpu
from jax.sharding import PartitionSpec as P

HOPS = 2
DOC_CAP = 4096
NEG = -1e30
MESH = pl.DeviceIdType.MESH
F32 = jnp.float32
BF16 = jnp.bfloat16


def dot(a, b, dims):
    return lax.dot_general(a, b, (dims, ((), ())), preferred_element_type=F32)


def kernel(
    n, heads_n, reach, docs,
    q_ref, k_ref, v_ref, g_ref, doc_ref, plan_ref,
    out_ref, dq_ref, dk_ref, dv_ref,
    kbuf, vbuf, scores, wb_scr, qs, gs, qt, gt,
    dk_out, dv_out, dk_in, dv_in, dk_own, dv_own, sum_out, sum_in,
    stage, win, pick, picked, plan_own, plan_far,
    kv_s, kv_r, dk_s, dk_r, win_s, win_r, pick_s, pick_r, plan_s, plan_r, sum_s, sum_r,
):
    tok, dh = k_ref.shape
    width = q_ref.shape[1]
    hh = width // dh
    half = tok // 2
    me = lax.axis_index("ctx")
    my_head = lax.axis_index("head")
    partner = me + 1 - 2 * lax.rem(me, 2)
    inv_root = 1.0 / math.sqrt(dh)
    factor = inv_root * math.log2(math.e)
    far = max(reach, HOPS)

    barrier = pltpu.get_barrier_semaphore()
    count = heads_n - 1
    for d in range(1, far + 1):
        count = count + jnp.where(me + d < n, 1, 0) + jnp.where(me >= d, 1, 0)

        @pl.when(me + d < n)
        def _():
            pl.semaphore_signal(barrier, inc=1, device_id={"ctx": me + d}, device_id_type=MESH)

        @pl.when(me >= d)
        def _():
            pl.semaphore_signal(barrier, inc=1, device_id={"ctx": me - d}, device_id_type=MESH)

    for o in range(1, heads_n):
        pl.semaphore_signal(
            barrier, inc=1, device_id={"head": lax.rem(my_head + o, heads_n)}, device_id_type=MESH
        )
    row = lax.broadcasted_iota(jnp.int32, plan_own.shape, 0)
    plan_own[...] = jnp.where(row == 0, plan_ref[0], plan_ref[1]).astype(F32)
    pl.semaphore_wait(barrier, count)

    def ctx_copy(src, dst, s, r, target):
        return pltpu.make_async_remote_copy(
            src_ref=src, dst_ref=dst, send_sem=s, recv_sem=r,
            device_id={"ctx": target}, device_id_type=MESH,
        )

    def k_copy(d):
        return ctx_copy(k_ref, kbuf.at[d - 1], kv_s.at[0, d - 1], kv_r.at[0, d - 1], me + d)

    def v_copy(d):
        return ctx_copy(v_ref, vbuf.at[d - 1], kv_s.at[1, d - 1], kv_r.at[1, d - 1], me + d)

    def dk_copy(d):
        return ctx_copy(dk_out.at[d - 1], dk_in.at[d - 1], dk_s.at[0, d - 1], dk_r.at[0, d - 1], me - d)

    def dv_copy(d):
        return ctx_copy(dv_out.at[d - 1], dv_in.at[d - 1], dk_s.at[1, d - 1], dk_r.at[1, d - 1], me - d)

    def win_copy(a, side):
        target = me + HOPS if side == 0 else me - HOPS
        return ctx_copy(stage.at[a], win.at[a, side], win_s.at[a, side], win_r.at[a, side], target)

    def pick_copy(a):
        return ctx_copy(pick.at[a], picked.at[a], pick_s.at[a], pick_r.at[a], partner)

    plan_copy = ctx_copy(plan_own, plan_far, plan_s, plan_r, partner)

    for d in range(1, reach + 1):

        @pl.when(me + d < n)
        def _():
            k_copy(d).start()
            v_copy(d).start()

    plan_copy.start()

    for h in range(hh):
        cols = slice(h * dh, (h + 1) * dh)
        rows = slice(h * tok, (h + 1) * tok)
        qh = q_ref[:, cols]
        gh = g_ref[:, cols]
        qs[rows, :] = qh
        gs[rows, :] = gh
        qt[:, rows] = qh.T
        gt[:, rows] = gh.T

    lanes = hh * tok
    place = me * tok + lax.rem(lax.broadcasted_iota(jnp.int32, (1, lanes), 1), tok)
    start = jnp.zeros((1, lanes), jnp.int32)
    bound = jnp.int32(0)
    for j in range(docs):
        bound = bound + doc_ref[j]
        start = jnp.where(bound <= place, bound, start)
    offset = lax.broadcasted_iota(jnp.int32, (tok, lanes), 0)

    def keys(d):
        return k_ref[...] if d == 0 else kbuf[d - 1]

    def values(d):
        return v_ref[...] if d == 0 else vbuf[d - 1]

    top = jnp.full((1, lanes), NEG, F32)
    for d in range(reach + 1):
        if d:

            @pl.when(me >= d)
            def _():
                k_copy(d).wait_recv()

            @pl.when(me < d)
            def _():
                kbuf[d - 1] = jnp.zeros((tok, dh), BF16)
                vbuf[d - 1] = jnp.zeros((tok, dh), BF16)

        raw = dot(keys(d), qt[...], ((1,), (0,)))
        t = offset + (me - d) * tok
        allowed = t >= start
        if d == 0:
            allowed = allowed & (t <= place)
        else:
            allowed = allowed & (t >= 0)
        raw = jnp.where(allowed, raw, NEG)
        scores[d] = raw
        top = jnp.maximum(top, jnp.max(raw, axis=0, keepdims=True))

    total = jnp.zeros((1, lanes), F32)
    for d in range(reach + 1):
        e = jnp.exp2((scores[d] - top) * factor)
        scores[d] = e
        total = total + jnp.sum(e, axis=0, keepdims=True)
    inverse = 1.0 / total

    att = jnp.zeros((dh, lanes), F32)
    for d in range(reach, -1, -1):
        if d:

            @pl.when(me >= d)
            def _():
                v_copy(d).wait_recv()

        wb = (scores[d] * inverse).astype(BF16)
        att = att + dot(values(d), wb, ((0,), (0,)))
        wb_scr[d] = wb
    att = att.astype(BF16)
    for h in range(hh):
        stage[0, :, h * dh:(h + 1) * dh] = att[:, h * tok:(h + 1) * tok].T

    def send_window(a):
        @pl.when(me + HOPS < n)
        def _():
            win_copy(a, 0).start()

        @pl.when(me >= HOPS)
        def _():
            win_copy(a, 1).start()

    send_window(0)
    dots = jnp.sum(gt[...].astype(F32) * att.astype(F32), axis=0, keepdims=True)

    grad = jnp.zeros((dh, lanes), F32)
    for d in range(reach, -1, -1):
        value_term = dot(wb_scr[d], gs[...], ((1,), (0,)))
        gw = dot(values(d), gt[...], ((1,), (0,)))
        ds = (scores[d] * inverse * (gw - dots)).astype(BF16)
        key_term = dot(ds, qs[...], ((1,), (0,))) * inv_root
        grad = grad + dot(keys(d), ds, ((0,), (0,)))
        if d:
            dv_out[d - 1] = value_term.astype(BF16)
            dk_out[d - 1] = key_term.astype(BF16)

            @pl.when(me >= d)
            def _():
                dv_copy(d).start()
                dk_copy(d).start()

        else:
            dv_own[...] = value_term
            dk_own[...] = key_term
    grad = (grad * inv_root).astype(BF16)
    for h in range(hh):
        stage[1, :, h * dh:(h + 1) * dh] = grad[:, h * tok:(h + 1) * tok].T
    send_window(1)

    plan_copy.wait_recv()
    side = lax.rem(me, 2)
    other = me + HOPS - 2 * HOPS * side
    for a in range(2):

        @pl.when(me >= HOPS)
        def _():
            win_copy(a, 0).wait_recv()

        @pl.when(me + HOPS < n)
        def _():
            win_copy(a, 1).wait_recv()

        for s in range(2):
            want = plan_far[s:s + 1, :]
            acc = jnp.zeros((half, width), F32)
            for p in range(2):
                rows = slice(p * half, (p + 1) * half)
                own = jnp.broadcast_to(want == (2 * me + p).astype(F32), (half, width))
                acc = jnp.where(own, stage[a, rows, :].astype(F32), acc)
                away = jnp.broadcast_to(want == (2 * other + p).astype(F32), (half, width))
                acc = jnp.where(away, win[a, 1 - side, rows, :].astype(F32), acc)
            pick[a, s * half:(s + 1) * half, :] = acc.astype(BF16)
        pick_copy(a).start()

    for d in range(1, reach + 1):

        @pl.when(me + d < n)
        def _():
            dv_copy(d).wait_recv()
            dv_own[...] += dv_in[d - 1].astype(F32)
            dk_copy(d).wait_recv()
            dk_own[...] += dk_in[d - 1].astype(F32)

    sum_out[0] = dk_own[...]
    sum_out[1] = dv_own[...]

    def sum_copy(o):
        return pltpu.make_async_remote_copy(
            src_ref=sum_out, dst_ref=sum_in.at[o - 1], send_sem=sum_s.at[o - 1], recv_sem=sum_r.at[o - 1],
            device_id={"head": lax.rem(my_head + o, heads_n)}, device_id_type=MESH,
        )

    for o in range(1, heads_n):
        sum_copy(o).start()

    for a in range(2):
        pick_copy(a).wait_recv()
        for s in range(2):
            want = plan_own[s:s + 1, :]
            rows_s = slice(s * half, (s + 1) * half)
            acc = picked[a, rows_s, :].astype(F32)
            for p in range(2):
                rows = slice(p * half, (p + 1) * half)
                for base, at in ((0, None), (-HOPS, 0), (HOPS, 1)):
                    src = stage[a, rows, :] if at is None else win[a, at, rows, :]
                    hit = jnp.broadcast_to(want == (2 * (me + base) + p).astype(F32), (half, width))
                    acc = jnp.where(hit, src.astype(F32), acc)
            if a == 0:
                out_ref[rows_s, :] = acc.astype(BF16)
            else:
                dq_ref[rows_s, :] = acc

    for o in range(1, heads_n):
        sum_copy(o).wait_recv()
    dk_ref[...] = sum_out[0] + sum(sum_in[o, 0] for o in range(heads_n - 1))
    dv_ref[...] = sum_out[1] + sum(sum_in[o, 1] for o in range(heads_n - 1))

    for d in range(1, reach + 1):

        @pl.when(me + d < n)
        def _():
            k_copy(d).wait_send()
            v_copy(d).wait_send()

        @pl.when(me >= d)
        def _():
            dk_copy(d).wait_send()
            dv_copy(d).wait_send()

    for a in range(2):

        @pl.when(me + HOPS < n)
        def _():
            win_copy(a, 0).wait_send()

        @pl.when(me >= HOPS)
        def _():
            win_copy(a, 1).wait_send()

        pick_copy(a).wait_send()
    plan_copy.wait_send()
    for o in range(1, heads_n):
        sum_copy(o).wait_send()


def per_device(queries, key_input, value_input, grad_out, doc_lengths, stretch_plan):
    tok, dh = key_input.shape
    width = queries.shape[1]
    hh = width // dh
    n = lax.axis_size("ctx")
    heads_n = lax.axis_size("head")
    reach = min(n - 1, min(DOC_CAP, tok * n // 4) // tok)
    docs = doc_lengths.shape[0]
    lanes = hh * tok
    vmem = pl.BlockSpec(memory_space=pltpu.VMEM)
    smem = pl.BlockSpec(memory_space=pltpu.SMEM)
    dma = pltpu.SemaphoreType.DMA
    return pl.pallas_call(
        functools.partial(kernel, n, heads_n, reach, docs),
        out_shape=(
            jax.ShapeDtypeStruct((tok, width), BF16),
            jax.ShapeDtypeStruct((tok, width), F32),
            jax.ShapeDtypeStruct((tok, dh), F32),
            jax.ShapeDtypeStruct((tok, dh), F32),
        ),
        in_specs=[vmem, vmem, vmem, vmem, smem, smem],
        out_specs=(vmem, vmem, vmem, vmem),
        scratch_shapes=[
            pltpu.VMEM((reach, tok, dh), BF16),
            pltpu.VMEM((reach, tok, dh), BF16),
            pltpu.VMEM((reach + 1, tok, lanes), F32),
            pltpu.VMEM((reach + 1, tok, lanes), BF16),
            pltpu.VMEM((lanes, dh), BF16),
            pltpu.VMEM((lanes, dh), BF16),
            pltpu.VMEM((dh, lanes), BF16),
            pltpu.VMEM((dh, lanes), BF16),
            pltpu.VMEM((reach, tok, dh), BF16),
            pltpu.VMEM((reach, tok, dh), BF16),
            pltpu.VMEM((reach, tok, dh), BF16),
            pltpu.VMEM((reach, tok, dh), BF16),
            pltpu.VMEM((tok, dh), F32),
            pltpu.VMEM((tok, dh), F32),
            pltpu.VMEM((2, tok, dh), F32),
            pltpu.VMEM((heads_n - 1, 2, tok, dh), F32),
            pltpu.VMEM((2, tok, width), BF16),
            pltpu.VMEM((2, 2, tok, width), BF16),
            pltpu.VMEM((2, tok, width), BF16),
            pltpu.VMEM((2, tok, width), BF16),
            pltpu.VMEM((8, width), F32),
            pltpu.VMEM((8, width), F32),
            dma((2, reach)), dma((2, reach)),
            dma((2, reach)), dma((2, reach)),
            dma((2, 2)), dma((2, 2)),
            dma((2,)), dma((2,)),
            dma, dma,
            dma((heads_n - 1,)), dma((heads_n - 1,)),
        ],
        compiler_params=pltpu.CompilerParams(
            collective_id=0, has_side_effects=True, vmem_limit_bytes=48 * 1024 * 1024
        ),
    )(queries, key_input, value_input, grad_out, doc_lengths, stretch_plan)


def solution(mesh):
    return jax.shard_map(
        per_device,
        mesh=mesh,
        in_specs=(
            P(("groups", "ctx"), "head"),
            P(("groups", "ctx"), None),
            P(("groups", "ctx"), None),
            P(("groups", "ctx"), "head"),
            P("groups"),
            P(("groups", "ctx")),
        ),
        out_specs=(
            P(("groups", "ctx"), "head"),
            P(("groups", "ctx"), "head"),
            P(("groups", "ctx"), None),
            P(("groups", "ctx"), None),
        ),
        check_vma=False,
    )
```

```python
import functools
import math

import jax
import jax.numpy as jnp
from jax import lax
from jax.experimental import pallas as pl
from jax.experimental.pallas import tpu as pltpu
from jax.sharding import PartitionSpec as P

HOPS = 2
DOC_CAP = 4096
VMEM_GRANT = 64000 * 1024
NEG = -1e30
MESH = pl.DeviceIdType.MESH
F32 = jnp.float32
BF16 = jnp.bfloat16


def dot(a, b, dims):
    return lax.dot_general(a, b, (dims, ((), ())), preferred_element_type=F32)


def kernel(
    n, heads_n, reach, docs,
    q_hbm, k_hbm, v_hbm, g_hbm, doc_hbm, plan_hbm,
    out_hbm, dq_hbm, dk_hbm, dv_hbm,
    out_ref, dq_ref, dk_ref, dv_ref, store_s,
    kbuf, vbuf, scores, wb_scr, qs, gs, qt, gt,
    dk_out, dv_out, dk_in, dv_in, dk_own, dv_own, sum_out, sum_in,
    stage, win, pick, picked, plan_own, plan_far,
    q_ref, k_ref, v_ref, g_ref, doc_ref, plan_ref, load_s,
    kv_s, kv_r, dk_s, dk_r, win_s, win_r, pick_s, pick_r, plan_s, plan_r, sum_s, sum_r,
):
    tok, dh = k_ref.shape
    width = q_ref.shape[1]
    hh = width // dh
    half = tok // 2
    me = lax.axis_index("ctx")
    my_head = lax.axis_index("head")
    partner = me + 1 - 2 * lax.rem(me, 2)
    inv_root = 1.0 / math.sqrt(dh)
    factor = inv_root * math.log2(math.e)
    far = max(reach, HOPS)

    loads = [
        pltpu.make_async_copy(src, dst, load_s.at[j])
        for j, (src, dst) in enumerate((
            (plan_hbm, plan_ref), (doc_hbm, doc_ref), (q_hbm, q_ref),
            (g_hbm, g_ref), (k_hbm, k_ref), (v_hbm, v_ref),
        ))
    ]
    for load in loads:
        load.start()

    barrier = pltpu.get_barrier_semaphore()
    count = heads_n - 1
    for d in range(1, far + 1):
        count = count + jnp.where(me + d < n, 1, 0) + jnp.where(me >= d, 1, 0)

        @pl.when(me + d < n)
        def _():
            pl.semaphore_signal(barrier, inc=1, device_id={"ctx": me + d}, device_id_type=MESH)

        @pl.when(me >= d)
        def _():
            pl.semaphore_signal(barrier, inc=1, device_id={"ctx": me - d}, device_id_type=MESH)

    for o in range(1, heads_n):
        pl.semaphore_signal(
            barrier, inc=1, device_id={"head": lax.rem(my_head + o, heads_n)}, device_id_type=MESH
        )
    pl.semaphore_wait(barrier, count)

    def ctx_copy(src, dst, s, r, target):
        return pltpu.make_async_remote_copy(
            src_ref=src, dst_ref=dst, send_sem=s, recv_sem=r,
            device_id={"ctx": target}, device_id_type=MESH,
        )

    def k_copy(d):
        return ctx_copy(k_hbm, kbuf.at[d - 1], kv_s.at[0, d - 1], kv_r.at[0, d - 1], me + d)

    def v_copy(d):
        return ctx_copy(v_hbm, vbuf.at[d - 1], kv_s.at[1, d - 1], kv_r.at[1, d - 1], me + d)

    def dk_copy(d):
        return ctx_copy(dk_out.at[d - 1], dk_in.at[d - 1], dk_s.at[0, d - 1], dk_r.at[0, d - 1], me - d)

    def dv_copy(d):
        return ctx_copy(dv_out.at[d - 1], dv_in.at[d - 1], dk_s.at[1, d - 1], dk_r.at[1, d - 1], me - d)

    def win_copy(a, side):
        target = me + HOPS if side == 0 else me - HOPS
        return ctx_copy(stage.at[a], win.at[a, side], win_s.at[a, side], win_r.at[a, side], target)

    def pick_copy(a):
        return ctx_copy(pick.at[a], picked.at[a], pick_s.at[a], pick_r.at[a], partner)

    plan_copy = ctx_copy(plan_own, plan_far, plan_s, plan_r, partner)

    for d in range(1, reach + 1):

        @pl.when(me + d < n)
        def _():
            k_copy(d).start()

    for d in range(1, reach + 1):

        @pl.when(me + d < n)
        def _():
            v_copy(d).start()

    for load in loads:
        load.wait()
    row = lax.broadcasted_iota(jnp.int32, plan_own.shape, 0)
    plan_own[...] = jnp.where(row == 0, plan_ref[0], plan_ref[1]).astype(F32)
    plan_copy.start()

    for h in range(hh):
        cols = slice(h * dh, (h + 1) * dh)
        rows = slice(h * tok, (h + 1) * tok)
        qh = q_ref[:, cols]
        gh = g_ref[:, cols]
        qs[rows, :] = qh
        gs[rows, :] = gh
        qt[:, rows] = qh.T
        gt[:, rows] = gh.T

    lanes = hh * tok
    place = me * tok + lax.rem(lax.broadcasted_iota(jnp.int32, (1, lanes), 1), tok)
    start = jnp.zeros((1, lanes), jnp.int32)
    bound = jnp.int32(0)
    for j in range(docs):
        bound = bound + doc_ref[j]
        start = jnp.where(bound <= place, bound, start)
    offset = lax.broadcasted_iota(jnp.int32, (tok, lanes), 0)

    def keys(d):
        return k_ref[...] if d == 0 else kbuf[d - 1]

    def values(d):
        return v_ref[...] if d == 0 else vbuf[d - 1]

    top = jnp.full((1, lanes), NEG, F32)
    for d in range(reach + 1):
        if d:

            @pl.when(me >= d)
            def _():
                k_copy(d).wait_recv()

            @pl.when(me < d)
            def _():
                kbuf[d - 1] = jnp.zeros((tok, dh), BF16)
                vbuf[d - 1] = jnp.zeros((tok, dh), BF16)

        raw = dot(keys(d), qt[...], ((1,), (0,)))
        t = offset + (me - d) * tok
        allowed = t >= start
        if d == 0:
            allowed = allowed & (t <= place)
        else:
            allowed = allowed & (t >= 0)
        raw = jnp.where(allowed, raw, NEG)
        scores[d] = raw
        top = jnp.maximum(top, jnp.max(raw, axis=0, keepdims=True))

    total = jnp.zeros((1, lanes), F32)
    for d in range(reach + 1):
        e = jnp.exp2((scores[d] - top) * factor)
        scores[d] = e
        total = total + jnp.sum(e, axis=0, keepdims=True)
    inverse = 1.0 / total

    att = jnp.zeros((dh, lanes), F32)
    for d in range(reach, -1, -1):
        if d:

            @pl.when(me >= d)
            def _():
                v_copy(d).wait_recv()

        wb = (scores[d] * inverse).astype(BF16)
        att = att + dot(values(d), wb, ((0,), (0,)))
        wb_scr[d] = wb
    att = att.astype(BF16)
    for h in range(hh):
        stage[0, :, h * dh:(h + 1) * dh] = att[:, h * tok:(h + 1) * tok].T

    def send_window(a):
        @pl.when(me + HOPS < n)
        def _():
            win_copy(a, 0).start()

        @pl.when(me >= HOPS)
        def _():
            win_copy(a, 1).start()

    send_window(0)
    dots = jnp.sum(gt[...].astype(F32) * att.astype(F32), axis=0, keepdims=True)

    grad = jnp.zeros((dh, lanes), F32)
    for d in range(reach, -1, -1):
        value_term = dot(wb_scr[d], gs[...], ((1,), (0,)))
        gw = dot(values(d), gt[...], ((1,), (0,)))
        ds = (scores[d] * inverse * (gw - dots)).astype(BF16)
        key_term = dot(ds, qs[...], ((1,), (0,))) * inv_root
        grad = grad + dot(keys(d), ds, ((0,), (0,)))
        if d:
            dv_out[d - 1] = value_term.astype(BF16)
            dk_out[d - 1] = key_term.astype(BF16)

            @pl.when(me >= d)
            def _():
                dv_copy(d).start()
                dk_copy(d).start()

        else:
            dv_own[...] = value_term
            dk_own[...] = key_term
    grad = (grad * inv_root).astype(BF16)
    for h in range(hh):
        stage[1, :, h * dh:(h + 1) * dh] = grad[:, h * tok:(h + 1) * tok].T
    send_window(1)

    plan_copy.wait_recv()
    side = lax.rem(me, 2)
    other = me + HOPS - 2 * HOPS * side
    for a in range(2):

        @pl.when(me >= HOPS)
        def _():
            win_copy(a, 0).wait_recv()

        @pl.when(me + HOPS < n)
        def _():
            win_copy(a, 1).wait_recv()

        for s in range(2):
            want = plan_far[s:s + 1, :]
            acc = jnp.zeros((half, width), F32)
            for p in range(2):
                rows = slice(p * half, (p + 1) * half)
                own = jnp.broadcast_to(want == (2 * me + p).astype(F32), (half, width))
                acc = jnp.where(own, stage[a, rows, :].astype(F32), acc)
                away = jnp.broadcast_to(want == (2 * other + p).astype(F32), (half, width))
                acc = jnp.where(away, win[a, 1 - side, rows, :].astype(F32), acc)
            pick[a, s * half:(s + 1) * half, :] = acc.astype(BF16)
        pick_copy(a).start()

    for d in range(1, reach + 1):

        @pl.when(me + d < n)
        def _():
            dv_copy(d).wait_recv()
            dv_own[...] += dv_in[d - 1].astype(F32)
            dk_copy(d).wait_recv()
            dk_own[...] += dk_in[d - 1].astype(F32)

    sum_out[0] = dk_own[...]
    sum_out[1] = dv_own[...]

    def sum_copy(o):
        return pltpu.make_async_remote_copy(
            src_ref=sum_out, dst_ref=sum_in.at[o - 1], send_sem=sum_s.at[o - 1], recv_sem=sum_r.at[o - 1],
            device_id={"head": lax.rem(my_head + o, heads_n)}, device_id_type=MESH,
        )

    for o in range(1, heads_n):
        sum_copy(o).start()
    stores = [
        pltpu.make_async_copy(src, dst, store_s.at[j])
        for j, (src, dst) in enumerate((
            (out_ref, out_hbm), (dq_ref, dq_hbm), (dk_ref, dk_hbm), (dv_ref, dv_hbm),
        ))
    ]

    for a in range(2):
        pick_copy(a).wait_recv()
        for s in range(2):
            want = plan_own[s:s + 1, :]
            rows_s = slice(s * half, (s + 1) * half)
            acc = picked[a, rows_s, :].astype(F32)
            for p in range(2):
                rows = slice(p * half, (p + 1) * half)
                for base, at in ((0, None), (-HOPS, 0), (HOPS, 1)):
                    src = stage[a, rows, :] if at is None else win[a, at, rows, :]
                    hit = jnp.broadcast_to(want == (2 * (me + base) + p).astype(F32), (half, width))
                    acc = jnp.where(hit, src.astype(F32), acc)
            if a == 0:
                out_ref[rows_s, :] = acc.astype(BF16)
            else:
                dq_ref[rows_s, :] = acc
        stores[a].start()

    for o in range(1, heads_n):
        sum_copy(o).wait_recv()
    dk_ref[...] = sum_out[0] + sum(sum_in[o, 0] for o in range(heads_n - 1))
    stores[2].start()
    dv_ref[...] = sum_out[1] + sum(sum_in[o, 1] for o in range(heads_n - 1))
    stores[3].start()

    for d in range(1, reach + 1):

        @pl.when(me + d < n)
        def _():
            k_copy(d).wait_send()
            v_copy(d).wait_send()

        @pl.when(me >= d)
        def _():
            dk_copy(d).wait_send()
            dv_copy(d).wait_send()

    for a in range(2):

        @pl.when(me + HOPS < n)
        def _():
            win_copy(a, 0).wait_send()

        @pl.when(me >= HOPS)
        def _():
            win_copy(a, 1).wait_send()

        pick_copy(a).wait_send()
    plan_copy.wait_send()
    for o in range(1, heads_n):
        sum_copy(o).wait_send()
    for store in stores:
        store.wait()


def write_out(a, b, c, d, a_out, b_out, c_out, d_out, sems):
    copies = [
        pltpu.make_async_copy(src, dst, sems.at[j])
        for j, (src, dst) in enumerate(((a, a_out), (b, b_out), (c, c_out), (d, d_out)))
    ]
    for copy in copies:
        copy.start()
    for copy in copies:
        copy.wait()


def per_device(queries, key_input, value_input, grad_out, doc_lengths, stretch_plan):
    tok, dh = key_input.shape
    width = queries.shape[1]
    hh = width // dh
    n = lax.axis_size("ctx")
    heads_n = lax.axis_size("head")
    reach = min(n - 1, min(DOC_CAP, tok * n // 4) // tok)
    docs = doc_lengths.shape[0]
    lanes = hh * tok
    hbm = pl.BlockSpec(memory_space=pltpu.HBM)
    dma = pltpu.SemaphoreType.DMA
    results = (
        jax.ShapeDtypeStruct((tok, width), BF16),
        jax.ShapeDtypeStruct((tok, width), F32),
        jax.ShapeDtypeStruct((tok, dh), F32),
        jax.ShapeDtypeStruct((tok, dh), F32),
    )
    held = pl.pallas_call(
        functools.partial(kernel, n, heads_n, reach, docs),
        out_shape=results,
        in_specs=[hbm] * 6,
        out_specs=(hbm,) * 4,
        scratch_shapes=[
            pltpu.VMEM((tok, width), BF16),
            pltpu.VMEM((tok, width), F32),
            pltpu.VMEM((tok, dh), F32),
            pltpu.VMEM((tok, dh), F32),
            dma((4,)),
            pltpu.VMEM((reach, tok, dh), BF16),
            pltpu.VMEM((reach, tok, dh), BF16),
            pltpu.VMEM((reach + 1, tok, lanes), F32),
            pltpu.VMEM((reach + 1, tok, lanes), BF16),
            pltpu.VMEM((lanes, dh), BF16),
            pltpu.VMEM((lanes, dh), BF16),
            pltpu.VMEM((dh, lanes), BF16),
            pltpu.VMEM((dh, lanes), BF16),
            pltpu.VMEM((reach, tok, dh), BF16),
            pltpu.VMEM((reach, tok, dh), BF16),
            pltpu.VMEM((reach, tok, dh), BF16),
            pltpu.VMEM((reach, tok, dh), BF16),
            pltpu.VMEM((tok, dh), F32),
            pltpu.VMEM((tok, dh), F32),
            pltpu.VMEM((2, tok, dh), F32),
            pltpu.VMEM((heads_n - 1, 2, tok, dh), F32),
            pltpu.VMEM((2, tok, width), BF16),
            pltpu.VMEM((2, 2, tok, width), BF16),
            pltpu.VMEM((2, tok, width), BF16),
            pltpu.VMEM((2, tok, width), BF16),
            pltpu.VMEM((8, width), F32),
            pltpu.VMEM((8, width), F32),
            pltpu.VMEM((tok, width), BF16),
            pltpu.VMEM((tok, dh), BF16),
            pltpu.VMEM((tok, dh), BF16),
            pltpu.VMEM((tok, width), BF16),
            pltpu.SMEM((docs,), jnp.int32),
            pltpu.SMEM((2,), jnp.int32),
            dma((6,)),
            dma((2, reach)), dma((2, reach)),
            dma((2, reach)), dma((2, reach)),
            dma((2, 2)), dma((2, 2)),
            dma((2,)), dma((2,)),
            dma, dma,
            dma((heads_n - 1,)), dma((heads_n - 1,)),
        ],
        compiler_params=pltpu.CompilerParams(
            collective_id=0, has_side_effects=True, vmem_limit_bytes=VMEM_GRANT
        ),
    )(queries, key_input, value_input, grad_out, doc_lengths, stretch_plan)
    return pl.pallas_call(
        write_out,
        out_shape=results,
        in_specs=[pl.BlockSpec(memory_space=pl.ANY)] * 4,
        out_specs=(hbm,) * 4,
        scratch_shapes=[dma((4,))],
        compiler_params=pltpu.CompilerParams(vmem_limit_bytes=VMEM_GRANT),
    )(*held)


def solution(mesh):
    return jax.shard_map(
        per_device,
        mesh=mesh,
        in_specs=(
            P(("groups", "ctx"), "head"),
            P(("groups", "ctx"), None),
            P(("groups", "ctx"), None),
            P(("groups", "ctx"), "head"),
            P("groups"),
            P(("groups", "ctx")),
        ),
        out_specs=(
            P(("groups", "ctx"), "head"),
            P(("groups", "ctx"), "head"),
            P(("groups", "ctx"), None),
            P(("groups", "ctx"), None),
        ),
        check_vma=False,
    )
```

```python
import functools
import math

import jax
import jax.numpy as jnp
from jax import lax
from jax.experimental import pallas as pl
from jax.experimental.pallas import tpu as pltpu
from jax.sharding import PartitionSpec as P

HOPS = 2
DOC_CAP = 4096
VMEM_GRANT = 64000 * 1024
NEG = -1e30
MESH = pl.DeviceIdType.MESH
F32 = jnp.float32
BF16 = jnp.bfloat16


def dot(a, b, dims):
    return lax.dot_general(a, b, (dims, ((), ())), preferred_element_type=F32)


def kernel(
    n, heads_n, reach, docs,
    q_hbm, k_hbm, v_hbm, g_hbm, doc_hbm, plan_hbm,
    out_hbm, dq_hbm, dk_hbm, dv_hbm,
    out_ref, dq_ref, store_s,
    kbuf, vbuf, scores, wb_scr, qs, gs, qt, gt,
    part, part_in, red_out, red_in, sums,
    stage, win, pick, picked, plan_own, plan_far,
    q_ref, k_ref, v_ref, g_ref, doc_ref, plan_ref, load_s,
    kv_s, kv_r, part_s, part_r, red_s, red_r, win_s, win_r, pick_s, pick_r, plan_s, plan_r, sum_s, sum_r,
):
    tok, dh = k_ref.shape
    width = q_ref.shape[1]
    hh = width // dh
    half = tok // 2
    me = lax.axis_index("ctx")
    my_head = lax.axis_index("head")
    partner = me + 1 - 2 * lax.rem(me, 2)
    inv_root = 1.0 / math.sqrt(dh)
    factor = inv_root * math.log2(math.e)
    far = max(reach, HOPS)

    loads = [
        pltpu.make_async_copy(src, dst, load_s.at[j])
        for j, (src, dst) in enumerate((
            (plan_hbm, plan_ref), (doc_hbm, doc_ref), (q_hbm, q_ref),
            (g_hbm, g_ref), (k_hbm, k_ref), (v_hbm, v_ref),
        ))
    ]
    for load in loads:
        load.start()

    barrier = pltpu.get_barrier_semaphore()
    count = heads_n - 1
    for d in range(1, far + 1):
        count = count + jnp.where(me + d < n, 1, 0) + jnp.where(me >= d, 1, 0)

        @pl.when(me + d < n)
        def _():
            pl.semaphore_signal(barrier, inc=1, device_id={"ctx": me + d}, device_id_type=MESH)

        @pl.when(me >= d)
        def _():
            pl.semaphore_signal(barrier, inc=1, device_id={"ctx": me - d}, device_id_type=MESH)

    for o in range(1, heads_n):
        pl.semaphore_signal(
            barrier, inc=1, device_id={"head": lax.rem(my_head + o, heads_n)}, device_id_type=MESH
        )
    pl.semaphore_wait(barrier, count)

    def ctx_copy(src, dst, s, r, target):
        return pltpu.make_async_remote_copy(
            src_ref=src, dst_ref=dst, send_sem=s, recv_sem=r,
            device_id={"ctx": target}, device_id_type=MESH,
        )

    def k_copy(d):
        return ctx_copy(k_hbm, kbuf.at[d - 1], kv_s.at[0, d - 1], kv_r.at[0, d - 1], me + d)

    def v_copy(d):
        return ctx_copy(v_hbm, vbuf.at[d - 1], kv_s.at[1, d - 1], kv_r.at[1, d - 1], me + d)

    def head_copy(src, dst, s, r):
        return pltpu.make_async_remote_copy(
            src_ref=src, dst_ref=dst, send_sem=s, recv_sem=r,
            device_id={"head": 1 - my_head}, device_id_type=MESH,
        )

    def part_copy(d):
        return head_copy(part.at[d, 1 - my_head], part_in.at[d], part_s.at[d], part_r.at[d])

    def red_copy(d):
        return ctx_copy(red_out.at[d - 1], red_in.at[d - 1], red_s.at[d - 1], red_r.at[d - 1], me - d)

    def win_copy(c, side):
        target = me + HOPS if side == 0 else me - HOPS
        return ctx_copy(stage.at[c], win.at[c, side], win_s.at[c, side], win_r.at[c, side], target)

    def pick_copy(c):
        return ctx_copy(pick.at[c], picked.at[c], pick_s.at[c], pick_r.at[c], partner)

    sum_copy = head_copy(sums.at[my_head], sums.at[my_head], sum_s, sum_r)
    plan_copy = ctx_copy(plan_own, plan_far, plan_s, plan_r, partner)

    for d in range(1, reach + 1):

        @pl.when(me + d < n)
        def _():
            k_copy(d).start()

    for d in range(1, reach + 1):

        @pl.when(me + d < n)
        def _():
            v_copy(d).start()

    for load in loads:
        load.wait()
    row = lax.broadcasted_iota(jnp.int32, plan_own.shape, 0)
    plan_own[...] = jnp.where(row == 0, plan_ref[0], plan_ref[1]).astype(F32)
    plan_copy.start()

    for h in range(hh):
        cols = slice(h * dh, (h + 1) * dh)
        rows = slice(h * tok, (h + 1) * tok)
        qh = q_ref[:, cols]
        gh = g_ref[:, cols]
        qs[rows, :] = qh
        gs[rows, :] = gh
        qt[:, rows] = qh.T
        gt[:, rows] = gh.T

    lanes = hh * tok
    place = me * tok + lax.rem(lax.broadcasted_iota(jnp.int32, (1, lanes), 1), tok)
    start = jnp.zeros((1, lanes), jnp.int32)
    bound = jnp.int32(0)
    for j in range(docs):
        bound = bound + doc_ref[j]
        start = jnp.where(bound <= place, bound, start)
    offset = lax.broadcasted_iota(jnp.int32, (tok, lanes), 0)

    def keys(d):
        return k_ref[...] if d == 0 else kbuf[d - 1]

    def values(d):
        return v_ref[...] if d == 0 else vbuf[d - 1]

    top = jnp.full((1, lanes), NEG, F32)
    for d in range(reach + 1):
        if d:

            @pl.when(me >= d)
            def _():
                k_copy(d).wait_recv()

            @pl.when(me < d)
            def _():
                kbuf[d - 1] = jnp.zeros((tok, dh), BF16)
                vbuf[d - 1] = jnp.zeros((tok, dh), BF16)

        raw = dot(keys(d), qt[...], ((1,), (0,)))
        t = offset + (me - d) * tok
        allowed = t >= start
        if d == 0:
            allowed = allowed & (t <= place)
        else:
            allowed = allowed & (t >= 0)
        raw = jnp.where(allowed, raw, NEG)
        scores[d] = raw
        top = jnp.maximum(top, jnp.max(raw, axis=0, keepdims=True))

    total = jnp.zeros((1, lanes), F32)
    for d in range(reach + 1):
        e = jnp.exp2((scores[d] - top) * factor)
        scores[d] = e
        total = total + jnp.sum(e, axis=0, keepdims=True)
    inverse = 1.0 / total

    att = jnp.zeros((dh, lanes), F32)
    for d in range(reach, -1, -1):
        if d:

            @pl.when(me >= d)
            def _():
                v_copy(d).wait_recv()

        wb = (scores[d] * inverse).astype(BF16)
        att = att + dot(values(d), wb, ((0,), (0,)))
        wb_scr[d] = wb
    att = att.astype(BF16)

    def send_window(c, rows):
        stage[c] = rows

        @pl.when(me + HOPS < n)
        def _():
            win_copy(c, 0).start()

        @pl.when(me >= HOPS)
        def _():
            win_copy(c, 1).start()

    for h in range(hh):
        send_window(h, att[:, h * tok:(h + 1) * tok].T)
    dots = jnp.sum(gt[...].astype(F32) * att.astype(F32), axis=0, keepdims=True)

    grad = jnp.zeros((dh, lanes), F32)
    for d in range(reach, -1, -1):
        value_term = dot(wb_scr[d], gs[...], ((1,), (0,)))
        gw = dot(values(d), gt[...], ((1,), (0,)))
        ds = (scores[d] * inverse * (gw - dots)).astype(BF16)
        key_term = dot(ds, qs[...], ((1,), (0,))) * inv_root
        grad = grad + dot(keys(d), ds, ((0,), (0,)))
        part[d, 0] = key_term
        part[d, 1] = value_term
        part_copy(d).start()
    for d in range(reach, 0, -1):
        part_copy(d).wait_recv()
        red_out[d - 1] = (part[d, my_head] + part_in[d]).astype(BF16)

        @pl.when(me >= d)
        def _():
            red_copy(d).start()

    grad = (grad * inv_root).astype(BF16)
    for h in range(hh):
        send_window(hh + h, grad[:, h * tok:(h + 1) * tok].T)

    plan_copy.wait_recv()
    side = lax.rem(me, 2)
    other = me + HOPS - 2 * HOPS * side
    for c in range(2 * hh):

        @pl.when(me >= HOPS)
        def _():
            win_copy(c, 0).wait_recv()

        @pl.when(me + HOPS < n)
        def _():
            win_copy(c, 1).wait_recv()

        for s in range(2):
            want = plan_far[s:s + 1, :]
            acc = jnp.zeros((half, dh), F32)
            for p in range(2):
                rows = slice(p * half, (p + 1) * half)
                own = jnp.broadcast_to(want == (2 * me + p).astype(F32), (half, dh))
                acc = jnp.where(own, stage[c, rows, :].astype(F32), acc)
                away = jnp.broadcast_to(want == (2 * other + p).astype(F32), (half, dh))
                acc = jnp.where(away, win[c, 1 - side, rows, :].astype(F32), acc)
            pick[c, s * half:(s + 1) * half, :] = acc.astype(BF16)
        pick_copy(c).start()

    part_copy(0).wait_recv()
    sums[my_head] = part[0, my_head] + part_in[0]
    for d in range(1, reach + 1):

        @pl.when(me + d < n)
        def _():
            red_copy(d).wait_recv()
            sums[my_head] += red_in[d - 1].astype(F32)

    sum_copy.start()
    stores = [
        pltpu.make_async_copy(src, dst, store_s.at[j])
        for j, (src, dst) in enumerate((
            (out_ref, out_hbm), (dq_ref, dq_hbm), (sums.at[0], dk_hbm), (sums.at[1], dv_hbm),
        ))
    ]

    for c in range(2 * hh):
        pick_copy(c).wait_recv()
        cols = slice((c % hh) * dh, (c % hh + 1) * dh)
        for s in range(2):
            want = plan_own[s:s + 1, :]
            rows_s = slice(s * half, (s + 1) * half)
            acc = picked[c, rows_s, :].astype(F32)
            for p in range(2):
                rows = slice(p * half, (p + 1) * half)
                for base, at in ((0, None), (-HOPS, 0), (HOPS, 1)):
                    src = stage[c, rows, :] if at is None else win[c, at, rows, :]
                    hit = jnp.broadcast_to(want == (2 * (me + base) + p).astype(F32), (half, dh))
                    acc = jnp.where(hit, src.astype(F32), acc)
            if c < hh:
                out_ref[rows_s, cols] = acc.astype(BF16)
            else:
                dq_ref[rows_s, cols] = acc
        if c == hh - 1:
            stores[0].start()
    stores[1].start()
    sum_copy.wait_recv()
    stores[2].start()
    stores[3].start()

    for d in range(1, reach + 1):

        @pl.when(me + d < n)
        def _():
            k_copy(d).wait_send()
            v_copy(d).wait_send()

        @pl.when(me >= d)
        def _():
            red_copy(d).wait_send()

    for d in range(reach + 1):
        part_copy(d).wait_send()
    for c in range(2 * hh):

        @pl.when(me + HOPS < n)
        def _():
            win_copy(c, 0).wait_send()

        @pl.when(me >= HOPS)
        def _():
            win_copy(c, 1).wait_send()

        pick_copy(c).wait_send()
    plan_copy.wait_send()
    sum_copy.wait_send()
    for store in stores:
        store.wait()


def write_out(a, b, c, d, a_out, b_out, c_out, d_out, a_buf, b_buf, c_buf, d_buf, in_sems, out_sems):
    ins = [
        pltpu.make_async_copy(src, dst, in_sems.at[j])
        for j, (src, dst) in enumerate(((a, a_buf), (b, b_buf), (c, c_buf), (d, d_buf)))
    ]
    outs = [
        pltpu.make_async_copy(src, dst, out_sems.at[j])
        for j, (src, dst) in enumerate(((a_buf, a_out), (b_buf, b_out), (c_buf, c_out), (d_buf, d_out)))
    ]
    for copy in ins:
        copy.start()
    for copy, onward in zip(ins, outs):
        copy.wait()
        onward.start()
    for copy in outs:
        copy.wait()


def per_device(queries, key_input, value_input, grad_out, doc_lengths, stretch_plan):
    tok, dh = key_input.shape
    width = queries.shape[1]
    hh = width // dh
    n = lax.axis_size("ctx")
    heads_n = lax.axis_size("head")
    reach = min(n - 1, min(DOC_CAP, tok * n // 4) // tok)
    docs = doc_lengths.shape[0]
    lanes = hh * tok
    hbm = pl.BlockSpec(memory_space=pltpu.HBM)
    dma = pltpu.SemaphoreType.DMA
    results = (
        jax.ShapeDtypeStruct((tok, width), BF16),
        jax.ShapeDtypeStruct((tok, width), F32),
        jax.ShapeDtypeStruct((tok, dh), F32),
        jax.ShapeDtypeStruct((tok, dh), F32),
    )
    held = pl.pallas_call(
        functools.partial(kernel, n, heads_n, reach, docs),
        out_shape=results,
        in_specs=[hbm] * 6,
        out_specs=(hbm,) * 4,
        scratch_shapes=[
            pltpu.VMEM((tok, width), BF16),
            pltpu.VMEM((tok, width), F32),
            dma((4,)),
            pltpu.VMEM((reach, tok, dh), BF16),
            pltpu.VMEM((reach, tok, dh), BF16),
            pltpu.VMEM((reach + 1, tok, lanes), F32),
            pltpu.VMEM((reach + 1, tok, lanes), BF16),
            pltpu.VMEM((lanes, dh), BF16),
            pltpu.VMEM((lanes, dh), BF16),
            pltpu.VMEM((dh, lanes), BF16),
            pltpu.VMEM((dh, lanes), BF16),
            pltpu.VMEM((reach + 1, 2, tok, dh), F32),
            pltpu.VMEM((reach + 1, tok, dh), F32),
            pltpu.VMEM((reach, tok, dh), BF16),
            pltpu.VMEM((reach, tok, dh), BF16),
            pltpu.VMEM((2, tok, dh), F32),
            pltpu.VMEM((2 * hh, tok, dh), BF16),
            pltpu.VMEM((2 * hh, 2, tok, dh), BF16),
            pltpu.VMEM((2 * hh, tok, dh), BF16),
            pltpu.VMEM((2 * hh, tok, dh), BF16),
            pltpu.VMEM((8, dh), F32),
            pltpu.VMEM((8, dh), F32),
            pltpu.VMEM((tok, width), BF16),
            pltpu.VMEM((tok, dh), BF16),
            pltpu.VMEM((tok, dh), BF16),
            pltpu.VMEM((tok, width), BF16),
            pltpu.SMEM((docs,), jnp.int32),
            pltpu.SMEM((2,), jnp.int32),
            dma((6,)),
            dma((2, reach)), dma((2, reach)),
            dma((reach + 1,)), dma((reach + 1,)),
            dma((reach,)), dma((reach,)),
            dma((2 * hh, 2)), dma((2 * hh, 2)),
            dma((2 * hh,)), dma((2 * hh,)),
            dma, dma,
            dma, dma,
        ],
        compiler_params=pltpu.CompilerParams(
            collective_id=0, has_side_effects=True, vmem_limit_bytes=VMEM_GRANT
        ),
    )(queries, key_input, value_input, grad_out, doc_lengths, stretch_plan)
    return pl.pallas_call(
        write_out,
        out_shape=results,
        in_specs=[pl.BlockSpec(memory_space=pl.ANY)] * 4,
        out_specs=(hbm,) * 4,
        scratch_shapes=[pltpu.VMEM(r.shape, r.dtype) for r in results] + [dma((4,)), dma((4,))],
        compiler_params=pltpu.CompilerParams(vmem_limit_bytes=VMEM_GRANT),
    )(*held)


def solution(mesh):
    return jax.shard_map(
        per_device,
        mesh=mesh,
        in_specs=(
            P(("groups", "ctx"), "head"),
            P(("groups", "ctx"), None),
            P(("groups", "ctx"), None),
            P(("groups", "ctx"), "head"),
            P("groups"),
            P(("groups", "ctx")),
        ),
        out_specs=(
            P(("groups", "ctx"), "head"),
            P(("groups", "ctx"), "head"),
            P(("groups", "ctx"), None),
            P(("groups", "ctx"), None),
        ),
        check_vma=False,
    )
```

```python
import functools
import math

import jax
import jax.numpy as jnp
from jax import lax
from jax.experimental import pallas as pl
from jax.experimental.pallas import tpu as pltpu
from jax.sharding import PartitionSpec as P

HOPS = 2
DOC_CAP = 4096
VMEM_GRANT = 40 * 1024 * 1024
NEG = -1e30
MESH = pl.DeviceIdType.MESH
F32 = jnp.float32
BF16 = jnp.bfloat16


def dot(a, b, dims):
    return lax.dot_general(a, b, (dims, ((), ())), preferred_element_type=F32)


def kernel(
    n, heads_n, reach, docs,
    q_hbm, k_hbm, v_hbm, g_hbm, doc_hbm, plan_hbm,
    out_ref, dq_ref, dk_ref, dv_ref,
    kbuf, vbuf, scores, wb_scr, ds_scr, gw_own, qs, gs, qt, gt,
    part, part_in, red_out, red_in, sums,
    stage, win, pick, picked, plan_own, plan_far,
    q_ref, k_ref, v_ref, g_ref, doc_ref, plan_ref, load_s,
    kv_s, kv_r, part_s, part_r, red_s, red_r, win_s, win_r, pick_s, pick_r, plan_s, plan_r, sum_s, sum_r,
):
    tok, dh = k_ref.shape
    width = q_ref.shape[1]
    hh = width // dh
    half = tok // 2
    me = lax.axis_index("ctx")
    my_head = lax.axis_index("head")
    partner = me + 1 - 2 * lax.rem(me, 2)
    inv_root = 1.0 / math.sqrt(dh)
    factor = inv_root * math.log2(math.e)
    far = max(reach, HOPS)

    loads = [
        pltpu.make_async_copy(src, dst, load_s.at[j])
        for j, (src, dst) in enumerate((
            (plan_hbm, plan_ref), (doc_hbm, doc_ref), (q_hbm, q_ref),
            (g_hbm, g_ref), (k_hbm, k_ref), (v_hbm, v_ref),
        ))
    ]
    for load in loads:
        load.start()

    barrier = pltpu.get_barrier_semaphore()
    count = heads_n - 1
    for d in range(1, far + 1):
        count = count + jnp.where(me + d < n, 1, 0) + jnp.where(me >= d, 1, 0)

        @pl.when(me + d < n)
        def _():
            pl.semaphore_signal(barrier, inc=1, device_id={"ctx": me + d}, device_id_type=MESH)

        @pl.when(me >= d)
        def _():
            pl.semaphore_signal(barrier, inc=1, device_id={"ctx": me - d}, device_id_type=MESH)

    for o in range(1, heads_n):
        pl.semaphore_signal(
            barrier, inc=1, device_id={"head": lax.rem(my_head + o, heads_n)}, device_id_type=MESH
        )
    pl.semaphore_wait(barrier, count)

    def ctx_copy(src, dst, s, r, target):
        return pltpu.make_async_remote_copy(
            src_ref=src, dst_ref=dst, send_sem=s, recv_sem=r,
            device_id={"ctx": target}, device_id_type=MESH,
        )

    def k_copy(d):
        return ctx_copy(k_hbm, kbuf.at[d - 1], kv_s.at[0, d - 1], kv_r.at[0, d - 1], me + d)

    def v_copy(d):
        return ctx_copy(v_hbm, vbuf.at[d - 1], kv_s.at[1, d - 1], kv_r.at[1, d - 1], me + d)

    def head_copy(src, dst, s, r):
        return pltpu.make_async_remote_copy(
            src_ref=src, dst_ref=dst, send_sem=s, recv_sem=r,
            device_id={"head": 1 - my_head}, device_id_type=MESH,
        )

    def part_copy(d):
        return head_copy(part.at[d, 1 - my_head], part_in.at[d], part_s.at[d], part_r.at[d])

    def red_copy(d):
        return ctx_copy(red_out.at[d - 1], red_in.at[d - 1], red_s.at[d - 1], red_r.at[d - 1], me - d)

    def win_copy(c, side):
        target = me + HOPS if side == 0 else me - HOPS
        return ctx_copy(stage.at[c], win.at[c, side], win_s.at[c, side], win_r.at[c, side], target)

    def pick_copy(c):
        return ctx_copy(pick.at[c], picked.at[c], pick_s.at[c], pick_r.at[c], partner)

    sum_copy = head_copy(sums.at[my_head], sums.at[my_head], sum_s, sum_r)
    plan_copy = ctx_copy(plan_own, plan_far, plan_s, plan_r, partner)

    for d in range(1, reach + 1):

        @pl.when(me + d < n)
        def _():
            k_copy(d).start()

    for d in range(1, reach + 1):

        @pl.when(me + d < n)
        def _():
            v_copy(d).start()

    for load in loads:
        load.wait()
    row = lax.broadcasted_iota(jnp.int32, plan_own.shape, 0)
    plan_own[...] = jnp.where(row == 0, plan_ref[0], plan_ref[1]).astype(F32)
    plan_copy.start()

    for h in range(hh):
        cols = slice(h * dh, (h + 1) * dh)
        rows = slice(h * tok, (h + 1) * tok)
        qh = q_ref[:, cols]
        gh = g_ref[:, cols]
        qs[rows, :] = qh
        gs[rows, :] = gh
        qt[:, rows] = qh.T
        gt[:, rows] = gh.T

    lanes = hh * tok
    place = me * tok + lax.rem(lax.broadcasted_iota(jnp.int32, (1, lanes), 1), tok)
    start = jnp.zeros((1, lanes), jnp.int32)
    bound = jnp.int32(0)
    for j in range(docs):
        bound = bound + doc_ref[j]
        start = jnp.where(bound <= place, bound, start)
    offset = lax.broadcasted_iota(jnp.int32, (tok, lanes), 0)

    def keys(d):
        return k_ref[...] if d == 0 else kbuf[d - 1]

    def values(d):
        return v_ref[...] if d == 0 else vbuf[d - 1]

    tops, totals = [], []
    for d in range(reach + 1):
        if d:

            @pl.when(me >= d)
            def _():
                k_copy(d).wait_recv()

            @pl.when(me < d)
            def _():
                kbuf[d - 1] = jnp.zeros((tok, dh), BF16)
                vbuf[d - 1] = jnp.zeros((tok, dh), BF16)

        raw = dot(keys(d), qt[...], ((1,), (0,)))
        t = offset + (me - d) * tok
        allowed = t >= start
        if d == 0:
            allowed = allowed & (t <= place)
        else:
            allowed = allowed & (t >= 0)
        raw = jnp.where(allowed, raw, NEG)
        block_top = jnp.max(raw, axis=0, keepdims=True)
        e = jnp.exp2((raw - block_top) * factor)
        scores[d] = e
        tops.append(block_top)
        totals.append(jnp.sum(e, axis=0, keepdims=True))
        if d == 0:
            gw_own[...] = dot(values(0), gt[...], ((1,), (0,)))
    top = functools.reduce(jnp.maximum, tops)
    scales = [jnp.exp2((block_top - top) * factor) for block_top in tops]
    inverse = 1.0 / sum(total * scale for total, scale in zip(totals, scales))
    scales = [scale * inverse for scale in scales]

    att = jnp.zeros((dh, lanes), F32)
    for d in range(reach + 1):
        if d:

            @pl.when(me >= d)
            def _():
                v_copy(d).wait_recv()

        wb = (scores[d] * scales[d]).astype(BF16)
        att = att + dot(values(d), wb, ((0,), (0,)))
        wb_scr[d] = wb
    att = att.astype(BF16)

    def send_window(c, rows):
        stage[c] = rows

        @pl.when(me + HOPS < n)
        def _():
            win_copy(c, 0).start()

        @pl.when(me >= HOPS)
        def _():
            win_copy(c, 1).start()

    for h in range(hh):
        send_window(h, att[:, h * tok:(h + 1) * tok].T)
    dots = jnp.sum(gt[...].astype(F32) * att.astype(F32), axis=0, keepdims=True)

    grad = jnp.zeros((dh, lanes), F32)
    for d in range(reach + 1):
        gw = gw_own[...] if d == 0 else dot(values(d), gt[...], ((1,), (0,)))
        ds = (scores[d] * scales[d] * (gw - dots)).astype(BF16)
        ds_scr[d] = ds
        grad = grad + dot(keys(d), ds, ((0,), (0,)))
    grad = (grad * inv_root).astype(BF16)
    for h in range(hh):
        send_window(hh + h, grad[:, h * tok:(h + 1) * tok].T)

    for d in range(reach, -1, -1):
        part[d, 0] = dot(ds_scr[d], qs[...], ((1,), (0,))) * inv_root
        part[d, 1] = dot(wb_scr[d], gs[...], ((1,), (0,)))
        part_copy(d).start()
    for d in range(reach, 0, -1):
        part_copy(d).wait_recv()
        red_out[d - 1] = (part[d, my_head] + part_in[d]).astype(BF16)

        @pl.when(me >= d)
        def _():
            red_copy(d).start()

    plan_copy.wait_recv()
    side = lax.rem(me, 2)
    other = me + HOPS - 2 * HOPS * side
    for c in range(2 * hh):

        @pl.when(me >= HOPS)
        def _():
            win_copy(c, 0).wait_recv()

        @pl.when(me + HOPS < n)
        def _():
            win_copy(c, 1).wait_recv()

        for s in range(2):
            want = plan_far[s:s + 1, :]
            acc = jnp.zeros((half, dh), F32)
            for p in range(2):
                rows = slice(p * half, (p + 1) * half)
                own = jnp.broadcast_to(want == (2 * me + p).astype(F32), (half, dh))
                acc = jnp.where(own, stage[c, rows, :].astype(F32), acc)
                away = jnp.broadcast_to(want == (2 * other + p).astype(F32), (half, dh))
                acc = jnp.where(away, win[c, 1 - side, rows, :].astype(F32), acc)
            pick[c, s * half:(s + 1) * half, :] = acc.astype(BF16)
        pick_copy(c).start()

    part_copy(0).wait_recv()
    sums[my_head] = part[0, my_head] + part_in[0]
    for d in range(1, reach + 1):

        @pl.when(me + d < n)
        def _():
            red_copy(d).wait_recv()
            sums[my_head] += red_in[d - 1].astype(F32)

    sum_copy.start()
    for c in range(2 * hh):
        pick_copy(c).wait_recv()
        cols = slice((c % hh) * dh, (c % hh + 1) * dh)
        for s in range(2):
            want = plan_own[s:s + 1, :]
            rows_s = slice(s * half, (s + 1) * half)
            acc = picked[c, rows_s, :].astype(F32)
            for p in range(2):
                rows = slice(p * half, (p + 1) * half)
                for base, at in ((0, None), (-HOPS, 0), (HOPS, 1)):
                    src = stage[c, rows, :] if at is None else win[c, at, rows, :]
                    hit = jnp.broadcast_to(want == (2 * (me + base) + p).astype(F32), (half, dh))
                    acc = jnp.where(hit, src.astype(F32), acc)
            if c < hh:
                out_ref[rows_s, cols] = acc.astype(BF16)
            else:
                dq_ref[rows_s, cols] = acc
    sum_copy.wait_recv()
    dk_ref[...] = sums[0]
    dv_ref[...] = sums[1]

    for d in range(1, reach + 1):

        @pl.when(me + d < n)
        def _():
            k_copy(d).wait_send()
            v_copy(d).wait_send()

        @pl.when(me >= d)
        def _():
            red_copy(d).wait_send()

    for d in range(reach + 1):
        part_copy(d).wait_send()
    for c in range(2 * hh):

        @pl.when(me + HOPS < n)
        def _():
            win_copy(c, 0).wait_send()

        @pl.when(me >= HOPS)
        def _():
            win_copy(c, 1).wait_send()

        pick_copy(c).wait_send()
    plan_copy.wait_send()
    sum_copy.wait_send()


def write_out(a, b, c, d, a_out, b_out, c_out, d_out, sems):
    copies = [
        pltpu.make_async_copy(src, dst, sems.at[j])
        for j, (src, dst) in enumerate(((a, a_out), (b, b_out), (c, c_out), (d, d_out)))
    ]
    for copy in copies:
        copy.start()
    for copy in copies:
        copy.wait()


def per_device(queries, key_input, value_input, grad_out, doc_lengths, stretch_plan):
    tok, dh = key_input.shape
    width = queries.shape[1]
    hh = width // dh
    n = lax.axis_size("ctx")
    heads_n = lax.axis_size("head")
    reach = min(n - 1, min(DOC_CAP, tok * n // 4) // tok)
    docs = doc_lengths.shape[0]
    lanes = hh * tok
    hbm = pl.BlockSpec(memory_space=pltpu.HBM)
    vmem = pl.BlockSpec(memory_space=pltpu.VMEM)
    dma = pltpu.SemaphoreType.DMA
    results = (
        jax.ShapeDtypeStruct((tok, width), BF16),
        jax.ShapeDtypeStruct((tok, width), F32),
        jax.ShapeDtypeStruct((tok, dh), F32),
        jax.ShapeDtypeStruct((tok, dh), F32),
    )
    held = pl.pallas_call(
        functools.partial(kernel, n, heads_n, reach, docs),
        out_shape=tuple(pltpu.VMEM(r.shape, r.dtype) for r in results),
        in_specs=[hbm] * 6,
        out_specs=(vmem,) * 4,
        scratch_shapes=[
            pltpu.VMEM((reach, tok, dh), BF16),
            pltpu.VMEM((reach, tok, dh), BF16),
            pltpu.VMEM((reach + 1, tok, lanes), F32),
            pltpu.VMEM((reach + 1, tok, lanes), BF16),
            pltpu.VMEM((reach + 1, tok, lanes), BF16),
            pltpu.VMEM((tok, lanes), F32),
            pltpu.VMEM((lanes, dh), BF16),
            pltpu.VMEM((lanes, dh), BF16),
            pltpu.VMEM((dh, lanes), BF16),
            pltpu.VMEM((dh, lanes), BF16),
            pltpu.VMEM((reach + 1, 2, tok, dh), F32),
            pltpu.VMEM((reach + 1, tok, dh), F32),
            pltpu.VMEM((reach, tok, dh), BF16),
            pltpu.VMEM((reach, tok, dh), BF16),
            pltpu.VMEM((2, tok, dh), F32),
            pltpu.VMEM((2 * hh, tok, dh), BF16),
            pltpu.VMEM((2 * hh, 2, tok, dh), BF16),
            pltpu.VMEM((2 * hh, tok, dh), BF16),
            pltpu.VMEM((2 * hh, tok, dh), BF16),
            pltpu.VMEM((8, dh), F32),
            pltpu.VMEM((8, dh), F32),
            pltpu.VMEM((tok, width), BF16),
            pltpu.VMEM((tok, dh), BF16),
            pltpu.VMEM((tok, dh), BF16),
            pltpu.VMEM((tok, width), BF16),
            pltpu.SMEM((docs,), jnp.int32),
            pltpu.SMEM((2,), jnp.int32),
            dma((6,)),
            dma((2, reach)), dma((2, reach)),
            dma((reach + 1,)), dma((reach + 1,)),
            dma((reach,)), dma((reach,)),
            dma((2 * hh, 2)), dma((2 * hh, 2)),
            dma((2 * hh,)), dma((2 * hh,)),
            dma, dma,
            dma, dma,
        ],
        compiler_params=pltpu.CompilerParams(
            collective_id=0, has_side_effects=True, vmem_limit_bytes=VMEM_GRANT
        ),
    )(*(
        pltpu.with_memory_space_constraint(arg, pltpu.HBM)
        for arg in (queries, key_input, value_input, grad_out, doc_lengths, stretch_plan)
    ))
    return pl.pallas_call(
        write_out,
        out_shape=results,
        in_specs=[vmem] * 4,
        out_specs=(hbm,) * 4,
        scratch_shapes=[dma((4,))],
        compiler_params=pltpu.CompilerParams(vmem_limit_bytes=VMEM_GRANT),
    )(*held)


def solution(mesh):
    return jax.shard_map(
        per_device,
        mesh=mesh,
        in_specs=(
            P(("groups", "ctx"), "head"),
            P(("groups", "ctx"), None),
            P(("groups", "ctx"), None),
            P(("groups", "ctx"), "head"),
            P("groups"),
            P(("groups", "ctx")),
        ),
        out_specs=(
            P(("groups", "ctx"), "head"),
            P(("groups", "ctx"), "head"),
            P(("groups", "ctx"), None),
            P(("groups", "ctx"), None),
        ),
        check_vma=False,
    )
```

```python
import functools
import math

import jax
import jax.numpy as jnp
from jax import lax
from jax.experimental import pallas as pl
from jax.experimental.pallas import tpu as pltpu
from jax.sharding import PartitionSpec as P

HOPS = 2
DOC_CAP = 4096
VMEM_GRANT = 40 * 1024 * 1024
NEG = -1e30
MESH = pl.DeviceIdType.MESH
F32 = jnp.float32
BF16 = jnp.bfloat16


def dot(a, b, dims):
    return lax.dot_general(a, b, (dims, ((), ())), preferred_element_type=F32)


def kernel(
    n, heads_n, reach, docs,
    q_hbm, k_hbm, v_hbm, g_hbm, doc_hbm, plan_hbm,
    out_ref, dq_ref, dk_ref, dv_ref,
    kbuf, vbuf, scores, wb_scr, ds_scr, gw_own, qs, gs, qt, gt,
    part, part_in, red_out, red_in, sums,
    stage, win, pick, picked, plan_own, plan_far,
    q_ref, k_ref, v_ref, g_ref, doc_ref, plan_ref, load_s,
    kv_s, kv_r, across_s, across_r, part_s, part_r, red_s, red_r, win_s, win_r, pick_s, pick_r, plan_s, plan_r, sum_s, sum_r,
):
    tok, dh = k_ref.shape
    width = q_ref.shape[1]
    hh = width // dh
    half = tok // 2
    me = lax.axis_index("ctx")
    my_head = lax.axis_index("head")
    partner = me + 1 - 2 * lax.rem(me, 2)
    inv_root = 1.0 / math.sqrt(dh)
    factor = inv_root * math.log2(math.e)
    far = max(reach, HOPS)

    loads = [
        pltpu.make_async_copy(src, dst, load_s.at[j])
        for j, (src, dst) in enumerate((
            (plan_hbm, plan_ref), (doc_hbm, doc_ref), (q_hbm, q_ref),
            (g_hbm, g_ref), (k_hbm, k_ref), (v_hbm, v_ref),
        ))
    ]
    for load in loads:
        load.start()

    barrier = pltpu.get_barrier_semaphore()
    count = heads_n - 1
    for d in range(1, far + 1):
        count = count + jnp.where(me + d < n, 1, 0) + jnp.where(me >= d, 1, 0)

        @pl.when(me + d < n)
        def _():
            pl.semaphore_signal(barrier, inc=1, device_id={"ctx": me + d}, device_id_type=MESH)

        @pl.when(me >= d)
        def _():
            pl.semaphore_signal(barrier, inc=1, device_id={"ctx": me - d}, device_id_type=MESH)

    for o in range(1, heads_n):
        pl.semaphore_signal(
            barrier, inc=1, device_id={"head": lax.rem(my_head + o, heads_n)}, device_id_type=MESH
        )
    pl.semaphore_wait(barrier, count)

    def ctx_copy(src, dst, s, r, target):
        return pltpu.make_async_remote_copy(
            src_ref=src, dst_ref=dst, send_sem=s, recv_sem=r,
            device_id={"ctx": target}, device_id_type=MESH,
        )

    def head_copy(src, dst, s, r):
        return pltpu.make_async_remote_copy(
            src_ref=src, dst_ref=dst, send_sem=s, recv_sem=r,
            device_id={"head": 1 - my_head}, device_id_type=MESH,
        )

    mine = pl.ds(pl.multiple_of(my_head * half, half), half)

    def k_copy(d):
        return ctx_copy(
            k_hbm.at[mine], kbuf.at[d - 1, mine], kv_s.at[0, d - 1], kv_r.at[0, d - 1], me + d
        )

    def v_copy(d):
        return ctx_copy(
            v_hbm.at[mine], vbuf.at[d - 1, mine], kv_s.at[1, d - 1], kv_r.at[1, d - 1], me + d
        )

    def k_across(d):
        rows = kbuf.at[d - 1, mine]
        return head_copy(rows, rows, across_s.at[0, d - 1], across_r.at[0, d - 1])

    def v_across(d):
        rows = vbuf.at[d - 1, mine]
        return head_copy(rows, rows, across_s.at[1, d - 1], across_r.at[1, d - 1])

    def part_copy(d):
        return head_copy(part.at[d, 1 - my_head], part_in.at[d], part_s.at[d], part_r.at[d])

    def red_copy(d):
        target = partner if d == 1 else me - d
        return ctx_copy(red_out.at[d - 1], red_in.at[d - 1], red_s.at[d - 1], red_r.at[d - 1], target)

    def win_copy(c, side):
        target = me + HOPS if side == 0 else me - HOPS
        return ctx_copy(stage.at[c], win.at[c, side], win_s.at[c, side], win_r.at[c, side], target)

    def pick_copy(c):
        return ctx_copy(pick.at[c], picked.at[c], pick_s.at[c], pick_r.at[c], partner)

    sum_copy = head_copy(sums.at[my_head], sums.at[my_head], sum_s, sum_r)
    plan_copy = ctx_copy(plan_own, plan_far, plan_s, plan_r, partner)

    for d in range(1, reach + 1):

        @pl.when(me + d < n)
        def _():
            k_copy(d).start()

    for d in range(1, reach + 1):

        @pl.when(me + d < n)
        def _():
            v_copy(d).start()

    for load in loads:
        load.wait()
    row = lax.broadcasted_iota(jnp.int32, plan_own.shape, 0)
    plan_own[...] = jnp.where(row == 0, plan_ref[0], plan_ref[1]).astype(F32)
    plan_copy.start()

    for h in range(hh):
        cols = slice(h * dh, (h + 1) * dh)
        rows = slice(h * tok, (h + 1) * tok)
        qh = q_ref[:, cols]
        gh = g_ref[:, cols]
        qs[rows, :] = qh
        gs[rows, :] = gh
        qt[:, rows] = qh.T
        gt[:, rows] = gh.T

    lanes = hh * tok
    place = me * tok + lax.rem(lax.broadcasted_iota(jnp.int32, (1, lanes), 1), tok)
    start = jnp.zeros((1, lanes), jnp.int32)
    bound = jnp.int32(0)
    for j in range(docs):
        bound = bound + doc_ref[j]
        start = jnp.where(bound <= place, bound, start)
    offset = lax.broadcasted_iota(jnp.int32, (tok, lanes), 0)

    def keys(d):
        return k_ref[...] if d == 0 else kbuf[d - 1]

    def values(d):
        return v_ref[...] if d == 0 else vbuf[d - 1]

    tops, totals = [], []
    for d in range(reach + 1):
        if d == 1:
            for b in range(1, reach + 1):

                @pl.when(me >= b)
                def _():
                    k_copy(b).wait_recv()
                    k_across(b).start()

                @pl.when(me < b)
                def _():
                    kbuf[b - 1] = jnp.zeros((tok, dh), BF16)
                    vbuf[b - 1] = jnp.zeros((tok, dh), BF16)

        if d == reach:
            for b in range(1, reach + 1):

                @pl.when(me >= b)
                def _():
                    v_copy(b).wait_recv()
                    v_across(b).start()

        if d:

            @pl.when(me >= d)
            def _():
                k_across(d).wait_recv()

        raw = dot(keys(d), qt[...], ((1,), (0,)))
        t = offset + (me - d) * tok
        allowed = t >= start
        if d == 0:
            allowed = allowed & (t <= place)
        else:
            allowed = allowed & (t >= 0)
        raw = jnp.where(allowed, raw, NEG)
        block_top = jnp.max(raw, axis=0, keepdims=True)
        e = jnp.exp2((raw - block_top) * factor)
        scores[d] = e
        tops.append(block_top)
        totals.append(jnp.sum(e, axis=0, keepdims=True))
        if d == 0:
            gw_own[...] = dot(values(0), gt[...], ((1,), (0,)))
    top = functools.reduce(jnp.maximum, tops)
    scales = [jnp.exp2((block_top - top) * factor) for block_top in tops]
    inverse = 1.0 / sum(total * scale for total, scale in zip(totals, scales))
    scales = [scale * inverse for scale in scales]

    att = jnp.zeros((dh, lanes), F32)
    for d in range(reach + 1):
        if d:

            @pl.when(me >= d)
            def _():
                v_across(d).wait_recv()

        wb = (scores[d] * scales[d]).astype(BF16)
        att = att + dot(values(d), wb, ((0,), (0,)))
        wb_scr[d] = wb
    att = att.astype(BF16)

    def send_window(c, rows):
        stage[c] = rows

        @pl.when(me + HOPS < n)
        def _():
            win_copy(c, 0).start()

        @pl.when(me >= HOPS)
        def _():
            win_copy(c, 1).start()

    for h in range(hh):
        send_window(h, att[:, h * tok:(h + 1) * tok].T)
    dots = jnp.sum(gt[...].astype(F32) * att.astype(F32), axis=0, keepdims=True)

    grad = jnp.zeros((dh, lanes), F32)
    for d in range(reach + 1):
        gw = gw_own[...] if d == 0 else dot(values(d), gt[...], ((1,), (0,)))
        ds = (scores[d] * scales[d] * (gw - dots)).astype(BF16)
        ds_scr[d] = ds
        grad = grad + dot(keys(d), ds, ((0,), (0,)))
    grad = (grad * inv_root).astype(BF16)
    for h in range(hh):
        send_window(hh + h, grad[:, h * tok:(h + 1) * tok].T)

    for d in range(1, reach + 2):
        d = d % (reach + 1)
        part[d, 0] = dot(ds_scr[d], qs[...], ((1,), (0,))) * inv_root
        part[d, 1] = dot(wb_scr[d], gs[...], ((1,), (0,)))
        part_copy(d).start()

    odd = lax.rem(me, 2) == 1
    for d in range(1, reach + 1):
        part_copy(d).wait_recv()
        term = part[d, my_head] + part_in[d]
        if d == 2:
            red_copy(1).wait_recv()
            term = term + jnp.where(odd, red_in[0].astype(F32), 0.0)
        red_out[d - 1] = term.astype(BF16)
        if d == 1:
            red_copy(d).start()
        else:

            @pl.when(me >= d)
            def _():
                red_copy(d).start()

    plan_copy.wait_recv()
    side = lax.rem(me, 2)
    other = me + HOPS - 2 * HOPS * side
    for c in range(2 * hh):

        @pl.when(me >= HOPS)
        def _():
            win_copy(c, 0).wait_recv()

        @pl.when(me + HOPS < n)
        def _():
            win_copy(c, 1).wait_recv()

        for s in range(2):
            want = plan_far[s:s + 1, :]
            acc = jnp.zeros((half, dh), F32)
            for p in range(2):
                rows = slice(p * half, (p + 1) * half)
                own = jnp.broadcast_to(want == (2 * me + p).astype(F32), (half, dh))
                acc = jnp.where(own, stage[c, rows, :].astype(F32), acc)
                away = jnp.broadcast_to(want == (2 * other + p).astype(F32), (half, dh))
                acc = jnp.where(away, win[c, 1 - side, rows, :].astype(F32), acc)
            pick[c, s * half:(s + 1) * half, :] = acc.astype(BF16)
        pick_copy(c).start()

    part_copy(0).wait_recv()
    sums[my_head] = part[0, my_head] + part_in[0]

    @pl.when(jnp.logical_not(odd))
    def _():
        sums[my_head] += red_in[0].astype(F32)

    for d in range(2, reach + 1):

        @pl.when(me + d < n)
        def _():
            red_copy(d).wait_recv()
            sums[my_head] += red_in[d - 1].astype(F32)

    sum_copy.start()
    for c in range(2 * hh):
        pick_copy(c).wait_recv()
        cols = slice((c % hh) * dh, (c % hh + 1) * dh)
        for s in range(2):
            want = plan_own[s:s + 1, :]
            rows_s = slice(s * half, (s + 1) * half)
            acc = picked[c, rows_s, :].astype(F32)
            for p in range(2):
                rows = slice(p * half, (p + 1) * half)
                for base, at in ((0, None), (-HOPS, 0), (HOPS, 1)):
                    src = stage[c, rows, :] if at is None else win[c, at, rows, :]
                    hit = jnp.broadcast_to(want == (2 * (me + base) + p).astype(F32), (half, dh))
                    acc = jnp.where(hit, src.astype(F32), acc)
            if c < hh:
                out_ref[rows_s, cols] = acc.astype(BF16)
            else:
                dq_ref[rows_s, cols] = acc
    sum_copy.wait_recv()
    dk_ref[...] = sums[0]
    dv_ref[...] = sums[1]

    for d in range(1, reach + 1):

        @pl.when(me + d < n)
        def _():
            k_copy(d).wait_send()
            v_copy(d).wait_send()

        @pl.when(me >= d)
        def _():
            k_across(d).wait_send()
            v_across(d).wait_send()

        if d == 1:
            red_copy(d).wait_send()
        else:

            @pl.when(me >= d)
            def _():
                red_copy(d).wait_send()

    for d in range(reach + 1):
        part_copy(d).wait_send()
    for c in range(2 * hh):

        @pl.when(me + HOPS < n)
        def _():
            win_copy(c, 0).wait_send()

        @pl.when(me >= HOPS)
        def _():
            win_copy(c, 1).wait_send()

        pick_copy(c).wait_send()
    plan_copy.wait_send()
    sum_copy.wait_send()


def write_out(a, b, c, d, a_out, b_out, c_out, d_out, sems):
    copies = [
        pltpu.make_async_copy(src, dst, sems.at[j])
        for j, (src, dst) in enumerate(((a, a_out), (b, b_out), (c, c_out), (d, d_out)))
    ]
    for copy in copies:
        copy.start()
    for copy in copies:
        copy.wait()


def per_device(queries, key_input, value_input, grad_out, doc_lengths, stretch_plan):
    tok, dh = key_input.shape
    width = queries.shape[1]
    hh = width // dh
    n = lax.axis_size("ctx")
    heads_n = lax.axis_size("head")
    reach = min(n - 1, min(DOC_CAP, tok * n // 4) // tok)
    docs = doc_lengths.shape[0]
    lanes = hh * tok
    hbm = pl.BlockSpec(memory_space=pltpu.HBM)
    vmem = pl.BlockSpec(memory_space=pltpu.VMEM)
    dma = pltpu.SemaphoreType.DMA
    results = (
        jax.ShapeDtypeStruct((tok, width), BF16),
        jax.ShapeDtypeStruct((tok, width), F32),
        jax.ShapeDtypeStruct((tok, dh), F32),
        jax.ShapeDtypeStruct((tok, dh), F32),
    )
    held = pl.pallas_call(
        functools.partial(kernel, n, heads_n, reach, docs),
        out_shape=tuple(pltpu.VMEM(r.shape, r.dtype) for r in results),
        in_specs=[hbm] * 6,
        out_specs=(vmem,) * 4,
        scratch_shapes=[
            pltpu.VMEM((reach, tok, dh), BF16),
            pltpu.VMEM((reach, tok, dh), BF16),
            pltpu.VMEM((reach + 1, tok, lanes), F32),
            pltpu.VMEM((reach + 1, tok, lanes), BF16),
            pltpu.VMEM((reach + 1, tok, lanes), BF16),
            pltpu.VMEM((tok, lanes), F32),
            pltpu.VMEM((lanes, dh), BF16),
            pltpu.VMEM((lanes, dh), BF16),
            pltpu.VMEM((dh, lanes), BF16),
            pltpu.VMEM((dh, lanes), BF16),
            pltpu.VMEM((reach + 1, 2, tok, dh), F32),
            pltpu.VMEM((reach + 1, tok, dh), F32),
            pltpu.VMEM((reach, tok, dh), BF16),
            pltpu.VMEM((reach, tok, dh), BF16),
            pltpu.VMEM((2, tok, dh), F32),
            pltpu.VMEM((2 * hh, tok, dh), BF16),
            pltpu.VMEM((2 * hh, 2, tok, dh), BF16),
            pltpu.VMEM((2 * hh, tok, dh), BF16),
            pltpu.VMEM((2 * hh, tok, dh), BF16),
            pltpu.VMEM((8, dh), F32),
            pltpu.VMEM((8, dh), F32),
            pltpu.VMEM((tok, width), BF16),
            pltpu.VMEM((tok, dh), BF16),
            pltpu.VMEM((tok, dh), BF16),
            pltpu.VMEM((tok, width), BF16),
            pltpu.SMEM((docs,), jnp.int32),
            pltpu.SMEM((2,), jnp.int32),
            dma((6,)),
            dma((2, reach)), dma((2, reach)),
            dma((2, reach)), dma((2, reach)),
            dma((reach + 1,)), dma((reach + 1,)),
            dma((reach,)), dma((reach,)),
            dma((2 * hh, 2)), dma((2 * hh, 2)),
            dma((2 * hh,)), dma((2 * hh,)),
            dma, dma,
            dma, dma,
        ],
        compiler_params=pltpu.CompilerParams(
            collective_id=0, has_side_effects=True, vmem_limit_bytes=VMEM_GRANT
        ),
    )(*(
        pltpu.with_memory_space_constraint(arg, pltpu.HBM)
        for arg in (queries, key_input, value_input, grad_out, doc_lengths, stretch_plan)
    ))
    return pl.pallas_call(
        write_out,
        out_shape=results,
        in_specs=[vmem] * 4,
        out_specs=(hbm,) * 4,
        scratch_shapes=[dma((4,))],
        compiler_params=pltpu.CompilerParams(vmem_limit_bytes=VMEM_GRANT),
    )(*held)


def solution(mesh):
    return jax.shard_map(
        per_device,
        mesh=mesh,
        in_specs=(
            P(("groups", "ctx"), "head"),
            P(("groups", "ctx"), None),
            P(("groups", "ctx"), None),
            P(("groups", "ctx"), "head"),
            P("groups"),
            P(("groups", "ctx")),
        ),
        out_specs=(
            P(("groups", "ctx"), "head"),
            P(("groups", "ctx"), "head"),
            P(("groups", "ctx"), None),
            P(("groups", "ctx"), None),
        ),
        check_vma=False,
    )
```

```python
import functools
import math

import jax
import jax.numpy as jnp
from jax import lax
from jax.experimental import pallas as pl
from jax.experimental.pallas import tpu as pltpu
from jax.sharding import PartitionSpec as P

HOPS = 2
DOC_CAP = 4096
VMEM_GRANT = 40 * 1024 * 1024
NEG = -1e30
MESH = pl.DeviceIdType.MESH
F32 = jnp.float32
BF16 = jnp.bfloat16


def dot(a, b, dims):
    return lax.dot_general(a, b, (dims, ((), ())), preferred_element_type=F32)


def kernel(
    n, heads_n, reach, docs,
    q_hbm, k_hbm, v_hbm, g_hbm, doc_hbm, plan_hbm,
    out_ref, dq_ref, dk_ref, dv_ref,
    kbuf, vbuf, scores, wb_scr, ds_scr, gw_own, qs, gs, qt, gt,
    part, part_in, red_out, red_in, sums,
    stage, win, pick, picked, plan_own, plan_far,
    q_ref, k_ref, v_ref, g_ref, doc_ref, plan_ref, load_s,
    kv_s, kv_r, part_s, part_r, red_s, red_r, win_s, win_r, pick_s, pick_r, plan_s, plan_r, sum_s, sum_r,
):
    tok, dh = k_ref.shape
    width = q_ref.shape[1]
    hh = width // dh
    half = tok // 2
    me = lax.axis_index("ctx")
    my_head = lax.axis_index("head")
    partner = me + 1 - 2 * lax.rem(me, 2)
    inv_root = 1.0 / math.sqrt(dh)
    factor = inv_root * math.log2(math.e)
    far = max(reach, HOPS)

    loads = [
        pltpu.make_async_copy(src, dst, load_s.at[j])
        for j, (src, dst) in enumerate((
            (plan_hbm, plan_ref), (doc_hbm, doc_ref), (q_hbm, q_ref),
            (g_hbm, g_ref), (k_hbm, k_ref), (v_hbm, v_ref),
        ))
    ]
    for load in loads:
        load.start()

    barrier = pltpu.get_barrier_semaphore()
    count = heads_n - 1
    for d in range(1, far + 1):
        count = count + jnp.where(me + d < n, 1, 0) + jnp.where(me >= d, 1, 0)

        @pl.when(me + d < n)
        def _():
            pl.semaphore_signal(barrier, inc=1, device_id={"ctx": me + d}, device_id_type=MESH)

        @pl.when(me >= d)
        def _():
            pl.semaphore_signal(barrier, inc=1, device_id={"ctx": me - d}, device_id_type=MESH)

    for o in range(1, heads_n):
        pl.semaphore_signal(
            barrier, inc=1, device_id={"head": lax.rem(my_head + o, heads_n)}, device_id_type=MESH
        )
    pl.semaphore_wait(barrier, count)

    def ctx_copy(src, dst, s, r, target):
        return pltpu.make_async_remote_copy(
            src_ref=src, dst_ref=dst, send_sem=s, recv_sem=r,
            device_id={"ctx": target}, device_id_type=MESH,
        )

    def head_copy(src, dst, s, r):
        return pltpu.make_async_remote_copy(
            src_ref=src, dst_ref=dst, send_sem=s, recv_sem=r,
            device_id={"head": 1 - my_head}, device_id_type=MESH,
        )

    def k_copy(d):
        return ctx_copy(k_hbm, kbuf.at[d - 1], kv_s.at[0, d - 1], kv_r.at[0, d - 1], me + d)

    def v_copy(d):
        return ctx_copy(v_hbm, vbuf.at[d - 1], kv_s.at[1, d - 1], kv_r.at[1, d - 1], me + d)

    def part_copy(d):
        return head_copy(part.at[d, 1 - my_head], part_in.at[d], part_s.at[d], part_r.at[d])

    def red_copy(d):
        target = partner if d == 1 else me - d
        return ctx_copy(red_out.at[d - 1], red_in.at[d - 1], red_s.at[d - 1], red_r.at[d - 1], target)

    def win_copy(c, side):
        target = me + HOPS if side == 0 else me - HOPS
        return ctx_copy(stage.at[c], win.at[c, side], win_s.at[c, side], win_r.at[c, side], target)

    def pick_copy(c):
        return ctx_copy(pick.at[c], picked.at[c], pick_s.at[c], pick_r.at[c], partner)

    sum_copy = head_copy(sums.at[my_head], sums.at[my_head], sum_s, sum_r)
    plan_copy = ctx_copy(plan_own, plan_far, plan_s, plan_r, partner)

    for d in range(1, reach + 1):

        @pl.when(me + d < n)
        def _():
            k_copy(d).start()

    for d in range(1, reach + 1):

        @pl.when(me + d < n)
        def _():
            v_copy(d).start()

    for load in loads:
        load.wait()
    row = lax.broadcasted_iota(jnp.int32, plan_own.shape, 0)
    plan_own[...] = jnp.where(row == 0, plan_ref[0], plan_ref[1]).astype(F32)
    plan_copy.start()

    for h in range(hh):
        cols = slice(h * dh, (h + 1) * dh)
        rows = slice(h * tok, (h + 1) * tok)
        qh = q_ref[:, cols]
        gh = g_ref[:, cols]
        qs[rows, :] = qh
        gs[rows, :] = gh
        qt[:, rows] = qh.T
        gt[:, rows] = gh.T

    lanes = hh * tok
    place = me * tok + lax.rem(lax.broadcasted_iota(jnp.int32, (1, lanes), 1), tok)
    start = jnp.zeros((1, lanes), jnp.int32)
    bound = jnp.int32(0)
    for j in range(docs):
        bound = bound + doc_ref[j]
        start = jnp.where(bound <= place, bound, start)
    offset = lax.broadcasted_iota(jnp.int32, (tok, lanes), 0)

    def keys(d):
        return k_ref[...] if d == 0 else kbuf[d - 1]

    def values(d):
        return v_ref[...] if d == 0 else vbuf[d - 1]

    tops, totals = [], []
    for d in range(reach + 1):
        if d:

            @pl.when(me >= d)
            def _():
                k_copy(d).wait_recv()

            @pl.when(me < d)
            def _():
                kbuf[d - 1] = jnp.zeros((tok, dh), BF16)
                vbuf[d - 1] = jnp.zeros((tok, dh), BF16)

        raw = dot(keys(d), qt[...], ((1,), (0,)))
        t = offset + (me - d) * tok
        allowed = t >= start
        if d == 0:
            allowed = allowed & (t <= place)
        else:
            allowed = allowed & (t >= 0)
        raw = jnp.where(allowed, raw, NEG)
        block_top = jnp.max(raw, axis=0, keepdims=True)
        e = jnp.exp2((raw - block_top) * factor)
        scores[d] = e
        tops.append(block_top)
        totals.append(jnp.sum(e, axis=0, keepdims=True))
        if d == 0:
            gw_own[...] = dot(values(0), gt[...], ((1,), (0,)))
    top = functools.reduce(jnp.maximum, tops)
    scales = [jnp.exp2((block_top - top) * factor) for block_top in tops]
    inverse = 1.0 / sum(total * scale for total, scale in zip(totals, scales))
    scales = [scale * inverse for scale in scales]

    att = jnp.zeros((dh, lanes), F32)
    for d in range(reach + 1):
        if d:

            @pl.when(me >= d)
            def _():
                v_copy(d).wait_recv()

        wb = (scores[d] * scales[d]).astype(BF16)
        att = att + dot(values(d), wb, ((0,), (0,)))
        wb_scr[d] = wb
    att = att.astype(BF16)

    def send_window(c, rows):
        stage[c] = rows

        @pl.when(me + HOPS < n)
        def _():
            win_copy(c, 0).start()

        @pl.when(me >= HOPS)
        def _():
            win_copy(c, 1).start()

    for h in range(hh):
        send_window(h, att[:, h * tok:(h + 1) * tok].T)
    dots = jnp.sum(gt[...].astype(F32) * att.astype(F32), axis=0, keepdims=True)

    grad = jnp.zeros((dh, lanes), F32)
    for d in range(reach + 1):
        gw = gw_own[...] if d == 0 else dot(values(d), gt[...], ((1,), (0,)))
        ds = (scores[d] * scales[d] * (gw - dots)).astype(BF16)
        ds_scr[d] = ds
        grad = grad + dot(keys(d), ds, ((0,), (0,)))
    grad = (grad * inv_root).astype(BF16)
    for h in range(hh):
        send_window(hh + h, grad[:, h * tok:(h + 1) * tok].T)

    for d in range(1, reach + 2):
        d = d % (reach + 1)
        part[d, 0] = dot(ds_scr[d], qs[...], ((1,), (0,))) * inv_root
        part[d, 1] = dot(wb_scr[d], gs[...], ((1,), (0,)))
        part_copy(d).start()

    plan_copy.wait_recv()
    side = lax.rem(me, 2)
    other = me + HOPS - 2 * HOPS * side
    def send_pick(c):

        @pl.when(me >= HOPS)
        def _():
            win_copy(c, 0).wait_recv()

        @pl.when(me + HOPS < n)
        def _():
            win_copy(c, 1).wait_recv()

        for s in range(2):
            want = plan_far[s:s + 1, :]
            acc = jnp.zeros((half, dh), F32)
            for p in range(2):
                rows = slice(p * half, (p + 1) * half)
                own = jnp.broadcast_to(want == (2 * me + p).astype(F32), (half, dh))
                acc = jnp.where(own, stage[c, rows, :].astype(F32), acc)
                away = jnp.broadcast_to(want == (2 * other + p).astype(F32), (half, dh))
                acc = jnp.where(away, win[c, 1 - side, rows, :].astype(F32), acc)
            pick[c, s * half:(s + 1) * half, :] = acc.astype(BF16)
        pick_copy(c).start()

    odd = lax.rem(me, 2) == 1
    for d in range(1, reach + 1):
        part_copy(d).wait_recv()
        term = part[d, my_head] + part_in[d]
        if d == 2:
            red_copy(1).wait_recv()
            term = term + jnp.where(odd, red_in[0].astype(F32), 0.0)
        red_out[d - 1] = term.astype(BF16)
        if d == 1:
            red_copy(d).start()
            for c in range(hh):
                send_pick(c)
        else:

            @pl.when(me >= d)
            def _():
                red_copy(d).start()

    for c in range(hh, 2 * hh):
        send_pick(c)

    part_copy(0).wait_recv()
    sums[my_head] = part[0, my_head] + part_in[0]

    @pl.when(jnp.logical_not(odd))
    def _():
        sums[my_head] += red_in[0].astype(F32)

    for d in range(2, reach + 1):

        @pl.when(me + d < n)
        def _():
            red_copy(d).wait_recv()
            sums[my_head] += red_in[d - 1].astype(F32)

    sum_copy.start()
    for c in range(2 * hh):
        pick_copy(c).wait_recv()
        cols = slice((c % hh) * dh, (c % hh + 1) * dh)
        for s in range(2):
            want = plan_own[s:s + 1, :]
            rows_s = slice(s * half, (s + 1) * half)
            acc = picked[c, rows_s, :].astype(F32)
            for p in range(2):
                rows = slice(p * half, (p + 1) * half)
                for base, at in ((0, None), (-HOPS, 0), (HOPS, 1)):
                    src = stage[c, rows, :] if at is None else win[c, at, rows, :]
                    hit = jnp.broadcast_to(want == (2 * (me + base) + p).astype(F32), (half, dh))
                    acc = jnp.where(hit, src.astype(F32), acc)
            if c < hh:
                out_ref[rows_s, cols] = acc.astype(BF16)
            else:
                dq_ref[rows_s, cols] = acc
    sum_copy.wait_recv()
    dk_ref[...] = sums[0]
    dv_ref[...] = sums[1]

    for d in range(1, reach + 1):

        @pl.when(me + d < n)
        def _():
            k_copy(d).wait_send()
            v_copy(d).wait_send()

        if d == 1:
            red_copy(d).wait_send()
        else:

            @pl.when(me >= d)
            def _():
                red_copy(d).wait_send()

    for d in range(reach + 1):
        part_copy(d).wait_send()
    for c in range(2 * hh):

        @pl.when(me + HOPS < n)
        def _():
            win_copy(c, 0).wait_send()

        @pl.when(me >= HOPS)
        def _():
            win_copy(c, 1).wait_send()

        pick_copy(c).wait_send()
    plan_copy.wait_send()
    sum_copy.wait_send()


def write_out(a, b, c, d, a_out, b_out, c_out, d_out, sems):
    copies = [
        pltpu.make_async_copy(src, dst, sems.at[j])
        for j, (src, dst) in enumerate(((a, a_out), (b, b_out), (c, c_out), (d, d_out)))
    ]
    for copy in copies:
        copy.start()
    for copy in copies:
        copy.wait()


def per_device(queries, key_input, value_input, grad_out, doc_lengths, stretch_plan):
    tok, dh = key_input.shape
    width = queries.shape[1]
    hh = width // dh
    n = lax.axis_size("ctx")
    heads_n = lax.axis_size("head")
    reach = min(n - 1, min(DOC_CAP, tok * n // 4) // tok)
    docs = doc_lengths.shape[0]
    lanes = hh * tok
    hbm = pl.BlockSpec(memory_space=pltpu.HBM)
    vmem = pl.BlockSpec(memory_space=pltpu.VMEM)
    dma = pltpu.SemaphoreType.DMA
    results = (
        jax.ShapeDtypeStruct((tok, width), BF16),
        jax.ShapeDtypeStruct((tok, width), F32),
        jax.ShapeDtypeStruct((tok, dh), F32),
        jax.ShapeDtypeStruct((tok, dh), F32),
    )
    held = pl.pallas_call(
        functools.partial(kernel, n, heads_n, reach, docs),
        out_shape=tuple(pltpu.VMEM(r.shape, r.dtype) for r in results),
        in_specs=[hbm] * 6,
        out_specs=(vmem,) * 4,
        scratch_shapes=[
            pltpu.VMEM((reach, tok, dh), BF16),
            pltpu.VMEM((reach, tok, dh), BF16),
            pltpu.VMEM((reach + 1, tok, lanes), F32),
            pltpu.VMEM((reach + 1, tok, lanes), BF16),
            pltpu.VMEM((reach + 1, tok, lanes), BF16),
            pltpu.VMEM((tok, lanes), F32),
            pltpu.VMEM((lanes, dh), BF16),
            pltpu.VMEM((lanes, dh), BF16),
            pltpu.VMEM((dh, lanes), BF16),
            pltpu.VMEM((dh, lanes), BF16),
            pltpu.VMEM((reach + 1, 2, tok, dh), F32),
            pltpu.VMEM((reach + 1, tok, dh), F32),
            pltpu.VMEM((reach, tok, dh), BF16),
            pltpu.VMEM((reach, tok, dh), BF16),
            pltpu.VMEM((2, tok, dh), F32),
            pltpu.VMEM((2 * hh, tok, dh), BF16),
            pltpu.VMEM((2 * hh, 2, tok, dh), BF16),
            pltpu.VMEM((2 * hh, tok, dh), BF16),
            pltpu.VMEM((2 * hh, tok, dh), BF16),
            pltpu.VMEM((8, dh), F32),
            pltpu.VMEM((8, dh), F32),
            pltpu.VMEM((tok, width), BF16),
            pltpu.VMEM((tok, dh), BF16),
            pltpu.VMEM((tok, dh), BF16),
            pltpu.VMEM((tok, width), BF16),
            pltpu.SMEM((docs,), jnp.int32),
            pltpu.SMEM((2,), jnp.int32),
            dma((6,)),
            dma((2, reach)), dma((2, reach)),
            dma((reach + 1,)), dma((reach + 1,)),
            dma((reach,)), dma((reach,)),
            dma((2 * hh, 2)), dma((2 * hh, 2)),
            dma((2 * hh,)), dma((2 * hh,)),
            dma, dma,
            dma, dma,
        ],
        compiler_params=pltpu.CompilerParams(
            collective_id=0, has_side_effects=True, vmem_limit_bytes=VMEM_GRANT
        ),
    )(*(
        pltpu.with_memory_space_constraint(arg, pltpu.HBM)
        for arg in (queries, key_input, value_input, grad_out, doc_lengths, stretch_plan)
    ))
    return pl.pallas_call(
        write_out,
        out_shape=results,
        in_specs=[vmem] * 4,
        out_specs=(hbm,) * 4,
        scratch_shapes=[dma((4,))],
        compiler_params=pltpu.CompilerParams(vmem_limit_bytes=VMEM_GRANT),
    )(*held)


def solution(mesh):
    return jax.shard_map(
        per_device,
        mesh=mesh,
        in_specs=(
            P(("groups", "ctx"), "head"),
            P(("groups", "ctx"), None),
            P(("groups", "ctx"), None),
            P(("groups", "ctx"), "head"),
            P("groups"),
            P(("groups", "ctx")),
        ),
        out_specs=(
            P(("groups", "ctx"), "head"),
            P(("groups", "ctx"), "head"),
            P(("groups", "ctx"), None),
            P(("groups", "ctx"), None),
        ),
        check_vma=False,
    )
```

```python
import functools
import math

import jax
import jax.numpy as jnp
from jax import lax
from jax.experimental import pallas as pl
from jax.experimental.pallas import tpu as pltpu
from jax.sharding import PartitionSpec as P

HOPS = 2
DOC_CAP = 4096
VMEM_GRANT = 40 * 1024 * 1024
NEG = -1e30
MESH = pl.DeviceIdType.MESH
F32 = jnp.float32
BF16 = jnp.bfloat16


def dot(a, b, dims):
    return lax.dot_general(a, b, (dims, ((), ())), preferred_element_type=F32)


def kernel(
    n, heads_n, reach, docs,
    q_hbm, k_hbm, v_hbm, g_hbm, doc_hbm, plan_hbm,
    out_ref, dq_ref, dk_ref, dv_ref,
    kbuf, vbuf, scores, wb_scr, ds_scr, gw_own, qs, gs, qt, gt,
    part, part_in, red_out, red_in, sums,
    stage, win, pick, picked, plan_own, plan_far,
    q_ref, k_ref, v_ref, g_ref, doc_ref, plan_ref, load_s,
    kv_s, kv_r, across_s, across_r, part_s, part_r, red_s, red_r, win_s, win_r, pick_s, pick_r, plan_s, plan_r, sum_s, sum_r,
):
    tok, dh = k_ref.shape
    width = q_ref.shape[1]
    hh = width // dh
    half = tok // 2
    me = lax.axis_index("ctx")
    my_head = lax.axis_index("head")
    partner = me + 1 - 2 * lax.rem(me, 2)
    inv_root = 1.0 / math.sqrt(dh)
    factor = inv_root * math.log2(math.e)
    far = max(reach, HOPS)

    loads = [
        pltpu.make_async_copy(src, dst, load_s.at[j])
        for j, (src, dst) in enumerate((
            (plan_hbm, plan_ref), (doc_hbm, doc_ref), (q_hbm, q_ref),
            (g_hbm, g_ref), (k_hbm, k_ref), (v_hbm, v_ref),
        ))
    ]
    for load in loads:
        load.start()

    barrier = pltpu.get_barrier_semaphore()
    count = heads_n - 1
    for d in range(1, far + 1):
        count = count + jnp.where(me + d < n, 1, 0) + jnp.where(me >= d, 1, 0)

        @pl.when(me + d < n)
        def _():
            pl.semaphore_signal(barrier, inc=1, device_id={"ctx": me + d}, device_id_type=MESH)

        @pl.when(me >= d)
        def _():
            pl.semaphore_signal(barrier, inc=1, device_id={"ctx": me - d}, device_id_type=MESH)

    for o in range(1, heads_n):
        pl.semaphore_signal(
            barrier, inc=1, device_id={"head": lax.rem(my_head + o, heads_n)}, device_id_type=MESH
        )
    pl.semaphore_wait(barrier, count)

    def ctx_copy(src, dst, s, r, target):
        return pltpu.make_async_remote_copy(
            src_ref=src, dst_ref=dst, send_sem=s, recv_sem=r,
            device_id={"ctx": target}, device_id_type=MESH,
        )

    def head_copy(src, dst, s, r):
        return pltpu.make_async_remote_copy(
            src_ref=src, dst_ref=dst, send_sem=s, recv_sem=r,
            device_id={"head": 1 - my_head}, device_id_type=MESH,
        )

    mine = pl.ds(pl.multiple_of(my_head * half, half), half)

    def k_copy(d):
        return ctx_copy(
            k_hbm.at[mine], kbuf.at[d - 1, mine], kv_s.at[0, d - 1], kv_r.at[0, d - 1], me + d
        )

    def v_copy(d):
        return ctx_copy(
            v_hbm.at[mine], vbuf.at[d - 1, mine], kv_s.at[1, d - 1], kv_r.at[1, d - 1], me + d
        )

    def k_across(d):
        rows = kbuf.at[d - 1, mine]
        return head_copy(rows, rows, across_s.at[0, d - 1], across_r.at[0, d - 1])

    def v_across(d):
        rows = vbuf.at[d - 1, mine]
        return head_copy(rows, rows, across_s.at[1, d - 1], across_r.at[1, d - 1])

    def part_copy(d):
        return head_copy(part.at[d, 1 - my_head], part_in.at[d], part_s.at[d], part_r.at[d])

    def red_copy(d):
        return ctx_copy(red_out.at[d - 1], red_in.at[d - 1], red_s.at[d - 1], red_r.at[d - 1], me - d)

    def win_copy(c, side):
        target = me + HOPS if side == 0 else me - HOPS
        return ctx_copy(stage.at[c], win.at[c, side], win_s.at[c, side], win_r.at[c, side], target)

    def pick_copy(c):
        return ctx_copy(pick.at[c], picked.at[c], pick_s.at[c], pick_r.at[c], partner)

    sum_copy = head_copy(sums.at[my_head], sums.at[my_head], sum_s, sum_r)
    plan_copy = ctx_copy(plan_own, plan_far, plan_s, plan_r, partner)

    for d in range(1, reach + 1):

        @pl.when(me + d < n)
        def _():
            k_copy(d).start()

    for d in range(1, reach + 1):

        @pl.when(me + d < n)
        def _():
            v_copy(d).start()

    for load in loads:
        load.wait()
    row = lax.broadcasted_iota(jnp.int32, plan_own.shape, 0)
    plan_own[...] = jnp.where(row == 0, plan_ref[0], plan_ref[1]).astype(F32)
    plan_copy.start()

    for h in range(hh):
        cols = slice(h * dh, (h + 1) * dh)
        rows = slice(h * tok, (h + 1) * tok)
        qh = q_ref[:, cols]
        gh = g_ref[:, cols]
        qs[rows, :] = qh
        gs[rows, :] = gh
        qt[:, rows] = qh.T
        gt[:, rows] = gh.T

    lanes = hh * tok
    place = me * tok + lax.rem(lax.broadcasted_iota(jnp.int32, (1, lanes), 1), tok)
    start = jnp.zeros((1, lanes), jnp.int32)
    bound = jnp.int32(0)
    for j in range(docs):
        bound = bound + doc_ref[j]
        start = jnp.where(bound <= place, bound, start)
    offset = lax.broadcasted_iota(jnp.int32, (tok, lanes), 0)

    def keys(d):
        return k_ref[...] if d == 0 else kbuf[d - 1]

    def values(d):
        return v_ref[...] if d == 0 else vbuf[d - 1]

    tops, totals = [], []
    for d in range(reach + 1):
        if d == 1:
            for b in range(1, reach + 1):

                @pl.when(me >= b)
                def _():
                    k_copy(b).wait_recv()
                    k_across(b).start()

                @pl.when(me < b)
                def _():
                    kbuf[b - 1] = jnp.zeros((tok, dh), BF16)
                    vbuf[b - 1] = jnp.zeros((tok, dh), BF16)

        if d == reach:
            for b in range(1, reach + 1):

                @pl.when(me >= b)
                def _():
                    v_copy(b).wait_recv()
                    v_across(b).start()

        if d:

            @pl.when(me >= d)
            def _():
                k_across(d).wait_recv()

        raw = dot(keys(d), qt[...], ((1,), (0,)))
        t = offset + (me - d) * tok
        allowed = t >= start
        if d == 0:
            allowed = allowed & (t <= place)
        else:
            allowed = allowed & (t >= 0)
        raw = jnp.where(allowed, raw, NEG)
        block_top = jnp.max(raw, axis=0, keepdims=True)
        e = jnp.exp2((raw - block_top) * factor)
        scores[d] = e
        tops.append(block_top)
        totals.append(jnp.sum(e, axis=0, keepdims=True))
        if d == 0:
            gw_own[...] = dot(values(0), gt[...], ((1,), (0,)))
    top = functools.reduce(jnp.maximum, tops)
    scales = [jnp.exp2((block_top - top) * factor) for block_top in tops]
    inverse = 1.0 / sum(total * scale for total, scale in zip(totals, scales))
    scales = [scale * inverse for scale in scales]

    att = jnp.zeros((dh, lanes), F32)
    for d in range(reach + 1):
        if d:

            @pl.when(me >= d)
            def _():
                v_across(d).wait_recv()

        wb = (scores[d] * scales[d]).astype(BF16)
        att = att + dot(values(d), wb, ((0,), (0,)))
        wb_scr[d] = wb
    att = att.astype(BF16)

    def send_window(c, rows):
        stage[c] = rows

        @pl.when(me + HOPS < n)
        def _():
            win_copy(c, 0).start()

        @pl.when(me >= HOPS)
        def _():
            win_copy(c, 1).start()

    for h in range(hh):
        send_window(h, att[:, h * tok:(h + 1) * tok].T)
    dots = jnp.sum(gt[...].astype(F32) * att.astype(F32), axis=0, keepdims=True)

    grad = jnp.zeros((dh, lanes), F32)
    for d in range(reach + 1):
        gw = gw_own[...] if d == 0 else dot(values(d), gt[...], ((1,), (0,)))
        ds = (scores[d] * scales[d] * (gw - dots)).astype(BF16)
        ds_scr[d] = ds
        grad = grad + dot(keys(d), ds, ((0,), (0,)))
    grad = (grad * inv_root).astype(BF16)
    for h in range(hh):
        send_window(hh + h, grad[:, h * tok:(h + 1) * tok].T)

    for d in range(reach, -1, -1):
        part[d, 0] = dot(ds_scr[d], qs[...], ((1,), (0,))) * inv_root
        part[d, 1] = dot(wb_scr[d], gs[...], ((1,), (0,)))
        part_copy(d).start()
    for d in range(reach, 0, -1):
        part_copy(d).wait_recv()
        red_out[d - 1] = (part[d, my_head] + part_in[d]).astype(BF16)

        @pl.when(me >= d)
        def _():
            red_copy(d).start()

    plan_copy.wait_recv()
    side = lax.rem(me, 2)
    other = me + HOPS - 2 * HOPS * side
    for c in range(2 * hh):

        @pl.when(me >= HOPS)
        def _():
            win_copy(c, 0).wait_recv()

        @pl.when(me + HOPS < n)
        def _():
            win_copy(c, 1).wait_recv()

        for s in range(2):
            want = plan_far[s:s + 1, :]
            acc = jnp.zeros((half, dh), F32)
            for p in range(2):
                rows = slice(p * half, (p + 1) * half)
                own = jnp.broadcast_to(want == (2 * me + p).astype(F32), (half, dh))
                acc = jnp.where(own, stage[c, rows, :].astype(F32), acc)
                away = jnp.broadcast_to(want == (2 * other + p).astype(F32), (half, dh))
                acc = jnp.where(away, win[c, 1 - side, rows, :].astype(F32), acc)
            pick[c, s * half:(s + 1) * half, :] = acc.astype(BF16)
        pick_copy(c).start()

    part_copy(0).wait_recv()
    sums[my_head] = part[0, my_head] + part_in[0]

    for d in range(1, reach + 1):

        @pl.when(me + d < n)
        def _():
            red_copy(d).wait_recv()
            sums[my_head] += red_in[d - 1].astype(F32)

    sum_copy.start()
    for c in range(2 * hh):
        pick_copy(c).wait_recv()
        cols = slice((c % hh) * dh, (c % hh + 1) * dh)
        for s in range(2):
            want = plan_own[s:s + 1, :]
            rows_s = slice(s * half, (s + 1) * half)
            acc = picked[c, rows_s, :].astype(F32)
            for p in range(2):
                rows = slice(p * half, (p + 1) * half)
                for base, at in ((0, None), (-HOPS, 0), (HOPS, 1)):
                    src = stage[c, rows, :] if at is None else win[c, at, rows, :]
                    hit = jnp.broadcast_to(want == (2 * (me + base) + p).astype(F32), (half, dh))
                    acc = jnp.where(hit, src.astype(F32), acc)
            if c < hh:
                out_ref[rows_s, cols] = acc.astype(BF16)
            else:
                dq_ref[rows_s, cols] = acc
    sum_copy.wait_recv()
    dk_ref[...] = sums[0]
    dv_ref[...] = sums[1]

    for d in range(1, reach + 1):

        @pl.when(me + d < n)
        def _():
            k_copy(d).wait_send()
            v_copy(d).wait_send()

        @pl.when(me >= d)
        def _():
            k_across(d).wait_send()
            v_across(d).wait_send()

        @pl.when(me >= d)
        def _():
            red_copy(d).wait_send()

    for d in range(reach + 1):
        part_copy(d).wait_send()
    for c in range(2 * hh):

        @pl.when(me + HOPS < n)
        def _():
            win_copy(c, 0).wait_send()

        @pl.when(me >= HOPS)
        def _():
            win_copy(c, 1).wait_send()

        pick_copy(c).wait_send()
    plan_copy.wait_send()
    sum_copy.wait_send()


def write_out(a, b, c, d, a_out, b_out, c_out, d_out, sems):
    copies = [
        pltpu.make_async_copy(src, dst, sems.at[j])
        for j, (src, dst) in enumerate(((a, a_out), (b, b_out), (c, c_out), (d, d_out)))
    ]
    for copy in copies:
        copy.start()
    for copy in copies:
        copy.wait()


def per_device(queries, key_input, value_input, grad_out, doc_lengths, stretch_plan):
    tok, dh = key_input.shape
    width = queries.shape[1]
    hh = width // dh
    n = lax.axis_size("ctx")
    heads_n = lax.axis_size("head")
    reach = min(n - 1, min(DOC_CAP, tok * n // 4) // tok)
    docs = doc_lengths.shape[0]
    lanes = hh * tok
    hbm = pl.BlockSpec(memory_space=pltpu.HBM)
    vmem = pl.BlockSpec(memory_space=pltpu.VMEM)
    dma = pltpu.SemaphoreType.DMA
    results = (
        jax.ShapeDtypeStruct((tok, width), BF16),
        jax.ShapeDtypeStruct((tok, width), F32),
        jax.ShapeDtypeStruct((tok, dh), F32),
        jax.ShapeDtypeStruct((tok, dh), F32),
    )
    held = pl.pallas_call(
        functools.partial(kernel, n, heads_n, reach, docs),
        out_shape=tuple(pltpu.VMEM(r.shape, r.dtype) for r in results),
        in_specs=[hbm] * 6,
        out_specs=(vmem,) * 4,
        scratch_shapes=[
            pltpu.VMEM((reach, tok, dh), BF16),
            pltpu.VMEM((reach, tok, dh), BF16),
            pltpu.VMEM((reach + 1, tok, lanes), F32),
            pltpu.VMEM((reach + 1, tok, lanes), BF16),
            pltpu.VMEM((reach + 1, tok, lanes), BF16),
            pltpu.VMEM((tok, lanes), F32),
            pltpu.VMEM((lanes, dh), BF16),
            pltpu.VMEM((lanes, dh), BF16),
            pltpu.VMEM((dh, lanes), BF16),
            pltpu.VMEM((dh, lanes), BF16),
            pltpu.VMEM((reach + 1, 2, tok, dh), F32),
            pltpu.VMEM((reach + 1, tok, dh), F32),
            pltpu.VMEM((reach, tok, dh), BF16),
            pltpu.VMEM((reach, tok, dh), BF16),
            pltpu.VMEM((2, tok, dh), F32),
            pltpu.VMEM((2 * hh, tok, dh), BF16),
            pltpu.VMEM((2 * hh, 2, tok, dh), BF16),
            pltpu.VMEM((2 * hh, tok, dh), BF16),
            pltpu.VMEM((2 * hh, tok, dh), BF16),
            pltpu.VMEM((8, dh), F32),
            pltpu.VMEM((8, dh), F32),
            pltpu.VMEM((tok, width), BF16),
            pltpu.VMEM((tok, dh), BF16),
            pltpu.VMEM((tok, dh), BF16),
            pltpu.VMEM((tok, width), BF16),
            pltpu.SMEM((docs,), jnp.int32),
            pltpu.SMEM((2,), jnp.int32),
            dma((6,)),
            dma((2, reach)), dma((2, reach)),
            dma((2, reach)), dma((2, reach)),
            dma((reach + 1,)), dma((reach + 1,)),
            dma((reach,)), dma((reach,)),
            dma((2 * hh, 2)), dma((2 * hh, 2)),
            dma((2 * hh,)), dma((2 * hh,)),
            dma, dma,
            dma, dma,
        ],
        compiler_params=pltpu.CompilerParams(
            collective_id=0, has_side_effects=True, vmem_limit_bytes=VMEM_GRANT
        ),
    )(*(
        pltpu.with_memory_space_constraint(arg, pltpu.HBM)
        for arg in (queries, key_input, value_input, grad_out, doc_lengths, stretch_plan)
    ))
    return pl.pallas_call(
        write_out,
        out_shape=results,
        in_specs=[vmem] * 4,
        out_specs=(hbm,) * 4,
        scratch_shapes=[dma((4,))],
        compiler_params=pltpu.CompilerParams(vmem_limit_bytes=VMEM_GRANT),
    )(*held)


def solution(mesh):
    return jax.shard_map(
        per_device,
        mesh=mesh,
        in_specs=(
            P(("groups", "ctx"), "head"),
            P(("groups", "ctx"), None),
            P(("groups", "ctx"), None),
            P(("groups", "ctx"), "head"),
            P("groups"),
            P(("groups", "ctx")),
        ),
        out_specs=(
            P(("groups", "ctx"), "head"),
            P(("groups", "ctx"), "head"),
            P(("groups", "ctx"), None),
            P(("groups", "ctx"), None),
        ),
        check_vma=False,
    )
```

```python
import functools
import math

import jax
import jax.numpy as jnp
from jax import lax
from jax.experimental import pallas as pl
from jax.experimental.pallas import tpu as pltpu
from jax.sharding import PartitionSpec as P

HOPS = 2
DOC_CAP = 4096
VMEM_GRANT = 40 * 1024 * 1024
NEG = -1e30
MESH = pl.DeviceIdType.MESH
F32 = jnp.float32
BF16 = jnp.bfloat16


def dot(a, b, dims):
    return lax.dot_general(a, b, (dims, ((), ())), preferred_element_type=F32)


def kernel(
    n, heads_n, reach, docs,
    q_hbm, k_hbm, v_hbm, g_hbm, doc_hbm, plan_hbm,
    out_ref, dq_ref, dk_ref, dv_ref,
    kbuf, vbuf, scores, wb_scr, ds_scr, gw_own, qs, gs, qt, gt,
    part, part_in, red_out, red_in, sums,
    stage, win, pick, picked, plan_own, plan_far,
    q_ref, k_ref, v_ref, g_ref, doc_ref, plan_ref, load_s,
    kv_s, kv_r, across_s, across_r, part_s, part_r, red_s, red_r, win_s, win_r, pick_s, pick_r, plan_s, plan_r, sum_s, sum_r,
):
    tok, dh = k_ref.shape
    width = q_ref.shape[1]
    hh = width // dh
    half = tok // 2
    me = lax.axis_index("ctx")
    my_head = lax.axis_index("head")
    partner = me + 1 - 2 * lax.rem(me, 2)
    inv_root = 1.0 / math.sqrt(dh)
    factor = inv_root * math.log2(math.e)
    far = max(reach, HOPS)

    loads = [
        pltpu.make_async_copy(src, dst, load_s.at[j])
        for j, (src, dst) in enumerate((
            (plan_hbm, plan_ref), (doc_hbm, doc_ref), (q_hbm, q_ref),
            (g_hbm, g_ref), (k_hbm, k_ref), (v_hbm, v_ref),
        ))
    ]
    for load in loads:
        load.start()

    barrier = pltpu.get_barrier_semaphore()
    count = heads_n - 1
    for d in range(1, far + 1):
        count = count + jnp.where(me + d < n, 1, 0) + jnp.where(me >= d, 1, 0)

        @pl.when(me + d < n)
        def _():
            pl.semaphore_signal(barrier, inc=1, device_id={"ctx": me + d}, device_id_type=MESH)

        @pl.when(me >= d)
        def _():
            pl.semaphore_signal(barrier, inc=1, device_id={"ctx": me - d}, device_id_type=MESH)

    for o in range(1, heads_n):
        pl.semaphore_signal(
            barrier, inc=1, device_id={"head": lax.rem(my_head + o, heads_n)}, device_id_type=MESH
        )
    pl.semaphore_wait(barrier, count)

    def ctx_copy(src, dst, s, r, target):
        return pltpu.make_async_remote_copy(
            src_ref=src, dst_ref=dst, send_sem=s, recv_sem=r,
            device_id={"ctx": target}, device_id_type=MESH,
        )

    def head_copy(src, dst, s, r):
        return pltpu.make_async_remote_copy(
            src_ref=src, dst_ref=dst, send_sem=s, recv_sem=r,
            device_id={"head": 1 - my_head}, device_id_type=MESH,
        )

    mine = pl.ds(pl.multiple_of(my_head * half, half), half)

    def k_copy(d):
        return ctx_copy(
            k_hbm.at[mine], kbuf.at[d - 1, mine], kv_s.at[0, d - 1], kv_r.at[0, d - 1], me + d
        )

    def v_copy(d):
        return ctx_copy(
            v_hbm.at[mine], vbuf.at[d - 1, mine], kv_s.at[1, d - 1], kv_r.at[1, d - 1], me + d
        )

    def k_across(d):
        rows = kbuf.at[d - 1, mine]
        return head_copy(rows, rows, across_s.at[0, d - 1], across_r.at[0, d - 1])

    def v_across(d):
        rows = vbuf.at[d - 1, mine]
        return head_copy(rows, rows, across_s.at[1, d - 1], across_r.at[1, d - 1])

    def part_copy(d):
        return head_copy(part.at[d, 1 - my_head], part_in.at[d], part_s.at[d], part_r.at[d])

    def red_copy(d):
        return ctx_copy(red_out.at[d - 1], red_in.at[d - 1], red_s.at[d - 1], red_r.at[d - 1], me - d)

    def win_copy(c, side):
        target = me + HOPS if side == 0 else me - HOPS
        return ctx_copy(stage.at[c], win.at[c, side], win_s.at[c, side], win_r.at[c, side], target)

    def pick_copy(c):
        return ctx_copy(pick.at[c], picked.at[c], pick_s.at[c], pick_r.at[c], partner)

    sum_copy = head_copy(sums.at[my_head], sums.at[my_head], sum_s, sum_r)
    plan_copy = ctx_copy(plan_own, plan_far, plan_s, plan_r, partner)

    for d in range(1, reach + 1):

        @pl.when(me + d < n)
        def _():
            k_copy(d).start()

    for d in range(1, reach + 1):

        @pl.when(me + d < n)
        def _():
            v_copy(d).start()

    for load in loads:
        load.wait()
    row = lax.broadcasted_iota(jnp.int32, plan_own.shape, 0)
    plan_own[...] = jnp.where(row == 0, plan_ref[0], plan_ref[1]).astype(F32)
    plan_copy.start()

    for h in range(hh):
        cols = slice(h * dh, (h + 1) * dh)
        rows = slice(h * tok, (h + 1) * tok)
        qh = q_ref[:, cols]
        gh = g_ref[:, cols]
        qs[rows, :] = qh
        gs[rows, :] = gh
        qt[:, rows] = qh.T
        gt[:, rows] = gh.T

    lanes = hh * tok
    place = me * tok + lax.rem(lax.broadcasted_iota(jnp.int32, (1, lanes), 1), tok)
    start = jnp.zeros((1, lanes), jnp.int32)
    bound = jnp.int32(0)
    for j in range(docs):
        bound = bound + doc_ref[j]
        start = jnp.where(bound <= place, bound, start)
    offset = lax.broadcasted_iota(jnp.int32, (tok, lanes), 0)

    def keys(d):
        return k_ref[...] if d == 0 else kbuf[d - 1]

    def values(d):
        return v_ref[...] if d == 0 else vbuf[d - 1]

    tops, totals = [], []
    for d in range(reach + 1):
        if d == 1:
            for b in range(1, reach + 1):

                @pl.when(me >= b)
                def _():
                    k_copy(b).wait_recv()
                    k_across(b).start()

                @pl.when(me < b)
                def _():
                    kbuf[b - 1] = jnp.zeros((tok, dh), BF16)
                    vbuf[b - 1] = jnp.zeros((tok, dh), BF16)

        if d == reach:
            for b in range(1, reach + 1):

                @pl.when(me >= b)
                def _():
                    v_copy(b).wait_recv()
                    v_across(b).start()

        if d:

            @pl.when(me >= d)
            def _():
                k_across(d).wait_recv()

        raw = dot(keys(d), qt[...], ((1,), (0,)))
        t = offset + (me - d) * tok
        allowed = t >= start
        if d == 0:
            allowed = allowed & (t <= place)
        else:
            allowed = allowed & (t >= 0)
        raw = jnp.where(allowed, raw, NEG)
        block_top = jnp.max(raw, axis=0, keepdims=True)
        e = jnp.exp2((raw - block_top) * factor)
        scores[d] = e
        tops.append(block_top)
        totals.append(jnp.sum(e, axis=0, keepdims=True))
        if d == 0:
            gw_own[...] = dot(values(0), gt[...], ((1,), (0,)))
    top = functools.reduce(jnp.maximum, tops)
    scales = [jnp.exp2((block_top - top) * factor) for block_top in tops]
    inverse = 1.0 / sum(total * scale for total, scale in zip(totals, scales))
    scales = [scale * inverse for scale in scales]

    for d in range(reach + 1):
        if d:

            @pl.when(me >= d)
            def _():
                v_across(d).wait_recv()

        wb = (scores[d] * scales[d]).astype(BF16)
        wb_scr[d] = wb
    def send_window(c, rows):
        stage[c] = rows

        @pl.when(me + HOPS < n)
        def _():
            win_copy(c, 0).start()

        @pl.when(me >= HOPS)
        def _():
            win_copy(c, 1).start()

    heads = []
    for h in range(hh):
        cols = slice(h * tok, (h + 1) * tok)
        terms = [dot(values(d), wb_scr[d, :, cols], ((0,), (0,))) for d in range(reach + 1)]
        heads.append(sum(terms).astype(BF16))
        send_window(h, heads[h].T)
    att = jnp.concatenate(heads, axis=1)
    dots = jnp.sum(gt[...].astype(F32) * att.astype(F32), axis=0, keepdims=True)

    grad = jnp.zeros((dh, lanes), F32)
    for d in range(reach + 1):
        gw = gw_own[...] if d == 0 else dot(values(d), gt[...], ((1,), (0,)))
        ds = (scores[d] * scales[d] * (gw - dots)).astype(BF16)
        ds_scr[d] = ds
        grad = grad + dot(keys(d), ds, ((0,), (0,)))
    grad = (grad * inv_root).astype(BF16)
    for h in range(hh):
        send_window(hh + h, grad[:, h * tok:(h + 1) * tok].T)

    for d in range(reach, -1, -1):
        part[d, 0] = dot(ds_scr[d], qs[...], ((1,), (0,))) * inv_root
        part[d, 1] = dot(wb_scr[d], gs[...], ((1,), (0,)))
        part_copy(d).start()
    for d in range(reach, 0, -1):
        part_copy(d).wait_recv()
        red_out[d - 1] = (part[d, my_head] + part_in[d]).astype(BF16)

        @pl.when(me >= d)
        def _():
            red_copy(d).start()

    plan_copy.wait_recv()
    side = lax.rem(me, 2)
    other = me + HOPS - 2 * HOPS * side
    for c in range(2 * hh):

        @pl.when(me >= HOPS)
        def _():
            win_copy(c, 0).wait_recv()

        @pl.when(me + HOPS < n)
        def _():
            win_copy(c, 1).wait_recv()

        for s in range(2):
            want = plan_far[s:s + 1, :]
            acc = jnp.zeros((half, dh), F32)
            for p in range(2):
                rows = slice(p * half, (p + 1) * half)
                own = jnp.broadcast_to(want == (2 * me + p).astype(F32), (half, dh))
                acc = jnp.where(own, stage[c, rows, :].astype(F32), acc)
                away = jnp.broadcast_to(want == (2 * other + p).astype(F32), (half, dh))
                acc = jnp.where(away, win[c, 1 - side, rows, :].astype(F32), acc)
            pick[c, s * half:(s + 1) * half, :] = acc.astype(BF16)
        pick_copy(c).start()

    part_copy(0).wait_recv()
    sums[my_head] = part[0, my_head] + part_in[0]

    for d in range(1, reach + 1):

        @pl.when(me + d < n)
        def _():
            red_copy(d).wait_recv()
            sums[my_head] += red_in[d - 1].astype(F32)

    sum_copy.start()
    for c in range(2 * hh):
        pick_copy(c).wait_recv()
        cols = slice((c % hh) * dh, (c % hh + 1) * dh)
        for s in range(2):
            want = plan_own[s:s + 1, :]
            rows_s = slice(s * half, (s + 1) * half)
            acc = picked[c, rows_s, :].astype(F32)
            for p in range(2):
                rows = slice(p * half, (p + 1) * half)
                for base, at in ((0, None), (-HOPS, 0), (HOPS, 1)):
                    src = stage[c, rows, :] if at is None else win[c, at, rows, :]
                    hit = jnp.broadcast_to(want == (2 * (me + base) + p).astype(F32), (half, dh))
                    acc = jnp.where(hit, src.astype(F32), acc)
            if c < hh:
                out_ref[rows_s, cols] = acc.astype(BF16)
            else:
                dq_ref[rows_s, cols] = acc
    sum_copy.wait_recv()
    dk_ref[...] = sums[0]
    dv_ref[...] = sums[1]

    for d in range(1, reach + 1):

        @pl.when(me + d < n)
        def _():
            k_copy(d).wait_send()
            v_copy(d).wait_send()

        @pl.when(me >= d)
        def _():
            k_across(d).wait_send()
            v_across(d).wait_send()

        @pl.when(me >= d)
        def _():
            red_copy(d).wait_send()

    for d in range(reach + 1):
        part_copy(d).wait_send()
    for c in range(2 * hh):

        @pl.when(me + HOPS < n)
        def _():
            win_copy(c, 0).wait_send()

        @pl.when(me >= HOPS)
        def _():
            win_copy(c, 1).wait_send()

        pick_copy(c).wait_send()
    plan_copy.wait_send()
    sum_copy.wait_send()


def write_out(a, b, c, d, a_out, b_out, c_out, d_out, sems):
    copies = [
        pltpu.make_async_copy(src, dst, sems.at[j])
        for j, (src, dst) in enumerate(((a, a_out), (b, b_out), (c, c_out), (d, d_out)))
    ]
    for copy in copies:
        copy.start()
    for copy in copies:
        copy.wait()


def per_device(queries, key_input, value_input, grad_out, doc_lengths, stretch_plan):
    tok, dh = key_input.shape
    width = queries.shape[1]
    hh = width // dh
    n = lax.axis_size("ctx")
    heads_n = lax.axis_size("head")
    reach = min(n - 1, min(DOC_CAP, tok * n // 4) // tok)
    docs = doc_lengths.shape[0]
    lanes = hh * tok
    hbm = pl.BlockSpec(memory_space=pltpu.HBM)
    vmem = pl.BlockSpec(memory_space=pltpu.VMEM)
    dma = pltpu.SemaphoreType.DMA
    results = (
        jax.ShapeDtypeStruct((tok, width), BF16),
        jax.ShapeDtypeStruct((tok, width), F32),
        jax.ShapeDtypeStruct((tok, dh), F32),
        jax.ShapeDtypeStruct((tok, dh), F32),
    )
    held = pl.pallas_call(
        functools.partial(kernel, n, heads_n, reach, docs),
        out_shape=tuple(pltpu.VMEM(r.shape, r.dtype) for r in results),
        in_specs=[hbm] * 6,
        out_specs=(vmem,) * 4,
        scratch_shapes=[
            pltpu.VMEM((reach, tok, dh), BF16),
            pltpu.VMEM((reach, tok, dh), BF16),
            pltpu.VMEM((reach + 1, tok, lanes), F32),
            pltpu.VMEM((reach + 1, tok, lanes), BF16),
            pltpu.VMEM((reach + 1, tok, lanes), BF16),
            pltpu.VMEM((tok, lanes), F32),
            pltpu.VMEM((lanes, dh), BF16),
            pltpu.VMEM((lanes, dh), BF16),
            pltpu.VMEM((dh, lanes), BF16),
            pltpu.VMEM((dh, lanes), BF16),
            pltpu.VMEM((reach + 1, 2, tok, dh), F32),
            pltpu.VMEM((reach + 1, tok, dh), F32),
            pltpu.VMEM((reach, tok, dh), BF16),
            pltpu.VMEM((reach, tok, dh), BF16),
            pltpu.VMEM((2, tok, dh), F32),
            pltpu.VMEM((2 * hh, tok, dh), BF16),
            pltpu.VMEM((2 * hh, 2, tok, dh), BF16),
            pltpu.VMEM((2 * hh, tok, dh), BF16),
            pltpu.VMEM((2 * hh, tok, dh), BF16),
            pltpu.VMEM((8, dh), F32),
            pltpu.VMEM((8, dh), F32),
            pltpu.VMEM((tok, width), BF16),
            pltpu.VMEM((tok, dh), BF16),
            pltpu.VMEM((tok, dh), BF16),
            pltpu.VMEM((tok, width), BF16),
            pltpu.SMEM((docs,), jnp.int32),
            pltpu.SMEM((2,), jnp.int32),
            dma((6,)),
            dma((2, reach)), dma((2, reach)),
            dma((2, reach)), dma((2, reach)),
            dma((reach + 1,)), dma((reach + 1,)),
            dma((reach,)), dma((reach,)),
            dma((2 * hh, 2)), dma((2 * hh, 2)),
            dma((2 * hh,)), dma((2 * hh,)),
            dma, dma,
            dma, dma,
        ],
        compiler_params=pltpu.CompilerParams(
            collective_id=0, has_side_effects=True, vmem_limit_bytes=VMEM_GRANT
        ),
    )(*(
        pltpu.with_memory_space_constraint(arg, pltpu.HBM)
        for arg in (queries, key_input, value_input, grad_out, doc_lengths, stretch_plan)
    ))
    return pl.pallas_call(
        write_out,
        out_shape=results,
        in_specs=[vmem] * 4,
        out_specs=(hbm,) * 4,
        scratch_shapes=[dma((4,))],
        compiler_params=pltpu.CompilerParams(vmem_limit_bytes=VMEM_GRANT),
    )(*held)


def solution(mesh):
    return jax.shard_map(
        per_device,
        mesh=mesh,
        in_specs=(
            P(("groups", "ctx"), "head"),
            P(("groups", "ctx"), None),
            P(("groups", "ctx"), None),
            P(("groups", "ctx"), "head"),
            P("groups"),
            P(("groups", "ctx")),
        ),
        out_specs=(
            P(("groups", "ctx"), "head"),
            P(("groups", "ctx"), "head"),
            P(("groups", "ctx"), None),
            P(("groups", "ctx"), None),
        ),
        check_vma=False,
    )
```
